32 devices in a mesh: sec: 4 (over z), gx: 2 (over x), gy: 4 (over y, core).
Axes of the slice: x: 2, y: 2, z: 4, core: 2. Of those that a mesh axis runs over, the one named last changes fastest.
Arguments:
- soil_class: int32 [64, 1024], P('gx', 'gy'), may hold values from 0 to 11
- geology_class: int32 [64, 1024], P('gx', 'gy'), may hold values from 0 to 15
- land_mask: int32 [64, 1024], P('gx', 'gy'), may hold values 0 or 1
- river_mask: int32 [64, 1024], P('gx', 'gy'), may hold values 0 or 1
- elevation: float32 [64, 1024], P('gx', 'gy'), may hold values from -6 to 6
- roughness: float32 [64, 1024], P('gx', 'gy'), may hold values from 0.02 to 0.11
- rainfall: float32 [64, 1024], P('gx', 'gy'), may hold values from 0.05 to 1
- potential_evap: float32 [64, 1024], P('gx', 'gy'), may hold values from 0.05 to 0.5
- surface_head: float32 [64, 1024], P('gx', 'gy'), may hold values from -3 to 3
- pressure: float32 [8, 64, 1024], P('sec', 'gx', 'gy'), may hold values from -6 to 6
- storage: float32 [8, 64, 1024], P('sec', 'gx', 'gy'), may hold values from 0.2 to 2
- soil_embed: bfloat16 [12, 128], replicated, may hold values from -4 to 4
- geology_embed: bfloat16 [16, 128], replicated, may hold values from -4 to 4
- conv_weight: bfloat16 [3, 3, 128, 128], replicated, may hold values from -0.1875 to 0.1875
- out_weight: bfloat16 [128, 8], replicated, may hold values from -0.5 to 0.5
Outputs:
- pressure_out: float32 [8, 64, 1024], P('sec', 'gx', 'gy')
- head_out: float32 [64, 1024], P('gx', 'gy')
The draws below stay inside these ranges and needn't reach their ends.
All inputs are finite; a program needn't handle non-finite values. No bound on the sum of `land_mask` or of `river_mask` on one device may be relied on, other than what follows from the above.
Results may differ from the reference program's by a relative error of at most 0.0041.
Values sent between devices are 32-bit elements; how exact they have to be, the bound alone decides.
A program may use at most 64 MiB of HBM per device.

```python
import math
import jax
import jax.numpy as jnp
from jax import lax

CX = 32
CHANNELS = 128
NSOIL = 12
NGEO = 16
SWEEPS = 4
CYCLES = 4
LAYERS = 8
NX = 64
NY = 1024
N_GX = 2


def set_ends(entries, rng, least, top_value):
    longest = entries.shape.index(max(entries.shape))
    spots = []
    for shift in (0, 1):
        where = [jax.random.randint(jax.random.fold_in(rng, axis), (), 0, length) for axis, length in enumerate(entries.shape)]
        where[longest] = (where[longest] + shift) % entries.shape[longest]
        spots.append(tuple(where))
    return entries.at[spots[0]].set(least).at[spots[1]].set(top_value)


def block_scale(stream_key, dims, pieces, least, high):
    gain = 1.0
    for axis_at, parts in pieces:
        draws = jax.random.uniform(jax.random.fold_in(jax.random.fold_in(stream_key, 6), axis_at), (parts,), jnp.float32, least / len(pieces), high / len(pieces))
        gain = gain * jnp.repeat(jnp.exp(draws), dims[axis_at] // parts).reshape((-1,) + (1,) * (len(dims) - 1 - axis_at))
    return gain


def gaussian(key, shape, width, limit, pieces=(), held_as=jnp.bfloat16):
    result = jax.random.normal(key, shape, jnp.float32) * width
    if len(pieces) > 0:
        result = block_scale(key, shape, pieces, -0.22, 0.18) * result
    return jnp.clip(result, min=-limit, max=limit).astype(held_as)


def setup_inputs(seed: int = 0) -> dict:
    streams_of = jax.random.split(jax.random.key(seed), 16)
    return {
        "soil_class": set_ends(jax.random.randint(streams_of[0], (NX, NY), 0, NSOIL), jax.random.fold_in(streams_of[0], 1), 0, NSOIL - 1).astype(jnp.int32),
        "geology_class": set_ends(jax.random.randint(streams_of[1], (NX, NY), 0, NGEO), jax.random.fold_in(streams_of[1], 1), 0, NGEO - 1).astype(jnp.int32),
        "land_mask": set_ends((jax.random.randint(streams_of[2], (NX, NY), 0, 5) < 4).astype(jnp.int32), jax.random.fold_in(streams_of[2], 1), 0, 1),
        "river_mask": set_ends((jax.random.randint(streams_of[3], (NX, NY), 0, 8) < 1).astype(jnp.int32), jax.random.fold_in(streams_of[3], 1), 0, 1),
        "elevation": gaussian(streams_of[4], (NX, NY), 1.0, 6.0, ((0, 2), (1, 4)), jnp.float32),
        "roughness": jnp.clip(jnp.exp(math.log(0.11) - 1.7047481 * jax.random.uniform(streams_of[5], (NX, NY), jnp.float32) ** block_scale(streams_of[5], (NX, NY), ((0, 2), (1, 4)), -0.2, 0.2)), 0.02, 0.11),
        "rainfall": jnp.clip(jnp.exp(math.log(1.0) - 2.9957323 * jax.random.uniform(streams_of[6], (NX, NY), jnp.float32) ** block_scale(streams_of[6], (NX, NY), ((0, 2), (1, 4)), -0.2, 0.2)), 0.05, 1.0),
        "potential_evap": jnp.clip(jnp.exp(math.log(0.5) - 2.3025851 * jax.random.uniform(streams_of[7], (NX, NY), jnp.float32) ** block_scale(streams_of[7], (NX, NY), ((0, 2), (1, 4)), -0.2, 0.2)), 0.05, 0.5),
        "surface_head": gaussian(streams_of[8], (NX, NY), 0.5, 3.0, ((0, 2), (1, 4)), jnp.float32),
        "pressure": gaussian(streams_of[9], (LAYERS, NX, NY), 1.0, 6.0, ((0, 4), (1, 2), (2, 4)), jnp.float32),
        "storage": jnp.clip(jnp.exp(math.log(2.0) - 2.3025851 * jax.random.uniform(streams_of[10], (LAYERS, NX, NY), jnp.float32) ** block_scale(streams_of[10], (LAYERS, NX, NY), ((0, 4), (1, 2), (2, 4)), -0.2, 0.2)), 0.2, 2.0),
        "soil_embed": gaussian(streams_of[11], (NSOIL, CHANNELS), 1.0, 4.0),
        "geology_embed": gaussian(streams_of[12], (NGEO, CHANNELS), 1.0, 4.0),
        "conv_weight": gaussian(streams_of[13], (3, 3, CHANNELS, CHANNELS), (9 * CHANNELS) ** -0.5, 0.1875),
        "out_weight": gaussian(streams_of[14], (CHANNELS, LAYERS), CHANNELS ** -0.5, 0.5),
    }


infil_rate = 0.3
lateral = 1.0
vertical = 0.5


def infiltration(land_frac, top_cond, surface, top_press):
    return land_frac * (infil_rate * top_cond / (1.0 + top_cond)) * (surface - top_press)


def evaporation_loss(land_frac, potential, top_press):
    return land_frac * potential * jax.nn.sigmoid(top_press)


def surface_flux(level_pad, rough_pad):
    centre_level = level_pad[1:-1, 1:-1]
    centre_rough = rough_pad[1:-1, 1:-1]
    total = jnp.zeros_like(centre_level)
    pairs = ((level_pad[2:, 1:-1], rough_pad[2:, 1:-1]), (level_pad[:-2, 1:-1], rough_pad[:-2, 1:-1]),
             (level_pad[1:-1, 2:], rough_pad[1:-1, 2:]), (level_pad[1:-1, :-2], rough_pad[1:-1, :-2]))
    for near_level, near_rough in pairs:
        total = total + 0.5 * (centre_rough + near_rough) * (near_level - centre_level)
    return total


def shifted(values):
    return [(values[:-2, 1:-1, 1:-1], vertical), (values[2:, 1:-1, 1:-1], vertical),
            (values[1:-1, :-2, 1:-1], lateral), (values[1:-1, 2:, 1:-1], lateral),
            (values[1:-1, 1:-1, 2:], lateral), (values[1:-1, 1:-1, :-2], lateral)]


def jacobi_sweep(press_pad, cond_pad, rhs_mid, store_mid):
    cond_mid = cond_pad[1:-1, 1:-1, 1:-1]
    diagonal = store_mid
    total = rhs_mid
    for (near_press, factor), (near_cond, unused) in zip(shifted(press_pad), shifted(cond_pad)):
        face = factor * 0.5 * (cond_mid + near_cond)
        diagonal = diagonal + face
        total = total + face * near_press
    return total / diagonal


def reference(soil_class, geology_class, land_mask, river_mask, elevation, roughness, rainfall, potential_evap,
              surface_head, pressure, storage, soil_embed, geology_embed, conv_weight, out_weight):
    soil_pad = jnp.pad(soil_class, 1, constant_values=-1)
    geology_pad = jnp.pad(geology_class, 1, constant_values=-1)
    soil_table = soil_embed.astype(jnp.float32)
    geology_table = geology_embed.astype(jnp.float32)
    kernel = conv_weight.astype(jnp.float32)
    projection = out_weight.astype(jnp.float32)

    def block_logits(index):
        start = (index * CX).astype(jnp.int32)
        soil_rows = lax.dynamic_slice_in_dim(soil_pad, start, CX + 2, 0)
        geology_rows = lax.dynamic_slice_in_dim(geology_pad, start, CX + 2, 0)
        soil_onehot = (soil_rows[:, :, None] == jnp.arange(NSOIL, dtype=jnp.int32)).astype(jnp.float32)
        geology_onehot = (geology_rows[:, :, None] == jnp.arange(NGEO, dtype=jnp.int32)).astype(jnp.float32)
        features = jnp.einsum("xys,sc->xyc", soil_onehot, soil_table) + jnp.einsum("xys,sc->xyc", geology_onehot, geology_table)
        features = features.astype(jnp.bfloat16).astype(jnp.float32)
        convolved = lax.conv_general_dilated(features[None], kernel, (1, 1), "VALID",
                                             dimension_numbers=("NHWC", "HWIO", "NCHW"),
                                             precision=lax.Precision.HIGHEST)[0]
        hidden = jax.nn.relu(convolved).astype(jnp.bfloat16).astype(jnp.float32)
        return jnp.einsum("cxy,cl->lxy", hidden, projection)

    blocks = lax.map(block_logits, jnp.arange(N_GX, dtype=jnp.int32))
    logits = jnp.transpose(blocks, (1, 0, 2, 3)).reshape(LAYERS, NX, NY)
    conduct = jnp.exp(logits)

    land_frac = land_mask.astype(jnp.float32)
    river_frac = river_mask.astype(jnp.float32)
    rough = land_frac * (1.0 + river_frac) * roughness
    rough_pad = jnp.pad(rough, 1)
    cond_pad = jnp.pad(conduct, 1)
    top_layer = (jnp.arange(LAYERS, dtype=jnp.int32) == 0).astype(jnp.float32)[:, None, None]
    surface = surface_head
    press = pressure
    for cycle in range(CYCLES):
        top_press = press[0]
        infil = infiltration(land_frac, conduct[0], surface, top_press)
        evap = evaporation_loss(land_frac, potential_evap, top_press)
        flux = surface_flux(jnp.pad(surface + elevation, 1), rough_pad)
        surface = surface + land_frac * (rainfall - infil + flux)
        source = infil - evap
        rhs = storage * press + top_layer * source[None]
        for sweep in range(SWEEPS):
            press = jacobi_sweep(jnp.pad(press, 1), cond_pad, rhs, storage)
    return press, surface
```

```python
import functools

import jax
import jax.numpy as jnp
from jax import lax
from jax.experimental import pallas as pl
from jax.experimental.pallas import tpu as pltpu
from jax.sharding import PartitionSpec as P

SWEEPS = 4
CYCLES = 4
REACH = SWEEPS * CYCLES
LANES = 128
TAPS = 3

infil_rate = 0.3
lateral = 1.0
vertical = 0.5
F32 = jnp.float32
MESH = pl.DeviceIdType.MESH


def iota(shape, axis):
    return lax.broadcasted_iota(jnp.int32, shape, axis)


def kernel(
    geom,
    soil_ref,
    geology_ref,
    land_ref,
    river_ref,
    elevation_ref,
    roughness_ref,
    rainfall_ref,
    potential_ref,
    head_ref,
    pressure_ref,
    storage_ref,
    soil_embed_ref,
    geology_embed_ref,
    conv_ref,
    outw_ref,
    press_out,
    head_out,
    cls,
    fld,
    pack2,
    halo2,
    stage3,
    win3,
    pack3,
    halo3,
    shifted_cls,
    table,
    taps,
    split,
    onehot,
    cond,
    coef,
    scaled,
    inverse,
    press_a,
    press_b,
    rhs,
    surf,
    send_out,
    recv_out,
    cls_send,
    cls_recv,
    fld_send,
    fld_recv,
    p2_send,
    p2_recv,
    s3_send,
    s3_recv,
    p3_send,
    p3_recv,
    out_send,
    out_recv,
):
    n_sec, n_gx, n_gy, rows, cols, layers_dev, win_rows = geom
    layers = n_sec * layers_dev
    own = cols // n_sec
    margin = (LANES - own) // 2
    groups = LANES // margin
    s, g, h = (
        jnp.clip(lax.axis_index(name), 0, size - 1) for name, size in (("sec", n_sec), ("gx", n_gx), ("gy", n_gy))
    )
    last = n_sec - 1
    extra = 8
    deep = REACH + extra

    def aligned(value):
        return pl.multiple_of(value, 8)

    offset = REACH

    def exists(dg, dh):
        return (g + dg >= 0) & (g + dg < n_gx) & (h + dh >= 0) & (h + dh < n_gy)

    lane = iota((rows, LANES), 1)
    turn = lax.rem(margin - own * s + cols, cols)

    def window_of(values):
        return pltpu.roll(values, turn, 1)[:, :LANES]

    land = land_ref[...].astype(F32)
    rough = land * (1.0 + river_ref[...].astype(F32)) * roughness_ref[...]
    classes = [soil_ref[...].astype(F32), geology_ref[...].astype(F32)]
    fields = [
        land,
        rough,
        elevation_ref[...],
        land * rainfall_ref[...],
        land * potential_ref[...],
        head_ref[...],
    ]
    windows = [window_of(v) for v in classes + fields]
    for k in range(2):
        cls[k, pl.ds(aligned(offset + extra), rows), :] = windows[k]
    for k in range(6):
        fld[k, pl.ds(aligned(offset), rows), :] = windows[2 + k]
    base = jnp.where(s == 0, 0, LANES - margin)
    for b in range(2):
        packed = jnp.zeros((rows, LANES), F32)
        for k in range(groups):
            moved = pltpu.roll(windows[b * groups + k], lax.rem(margin * k - base + LANES, LANES), 1)
            packed = jnp.where((lane >= margin * k) & (lane < margin * (k + 1)), moved, packed)
        pack2[b] = packed

    barrier = pltpu.get_barrier_semaphore()
    count = jnp.int32(0)
    for dg in (-1, 0, 1):
        for dh in (-1, 0, 1):
            for t in range(n_sec):
                met = exists(dg, dh)
                if dh == 0 and dg == 0:
                    met = met & (s != t)
                if dh == 1 and t != 0:
                    met = met & (s == last)
                if dh == -1 and t != last:
                    met = met & (s == 0)

                @pl.when(met)
                def _():
                    pl.semaphore_signal(
                        barrier, inc=1, device_id={"sec": t, "gx": g + dg, "gy": h + dh}, device_id_type=MESH
                    )

                count = count + met.astype(jnp.int32)

    soil_blocks = [pressure_ref[k] for k in range(layers_dev)] + [storage_ref[k] for k in range(layers_dev)]
    n_blocks = len(soil_blocks)
    for t in range(n_sec):
        for k in range(n_blocks):
            stage3[t, k] = pltpu.roll(soil_blocks[k], (margin - own * t) % cols, 1)[:, :LANES]
    for side, (t, edge) in enumerate(((0, 0), (last, LANES - margin))):
        packed = jnp.zeros((rows, LANES), F32)
        for k in range(n_blocks):
            moved = pltpu.roll(stage3[t, k], (margin * k - edge) % LANES, 1)
            packed = jnp.where((lane >= margin * k) & (lane < margin * (k + 1)), moved, packed)
        pack3[side] = packed
    for t in range(n_sec):

        @pl.when(s == t)
        def _():
            for k in range(n_blocks):
                win3[t, k, pl.ds(aligned(offset), rows), :] = stage3[t, k]


    pl.semaphore_wait(barrier, count)

    def source_rows(dg, size):
        return pl.ds(rows - size if dg == 1 else 0, size)

    def target_rows(dg, pad, size):
        if dg == 0:
            return pl.ds(aligned(offset + pad), size)
        if dg == 1:
            return pl.ds(REACH + pad - size, size)
        return pl.ds(REACH + rows + pad, size)

    def giver_rows(dg, pad, size):
        if dg == 1:
            return pl.ds(REACH + pad + rows - size, size)
        return pl.ds(REACH + pad, size)

    sends = []
    recvs = {"first": [], "soil": [], "rest": []}

    def message(kind, send_when, recv_when, src, dst, recv_dst, ssem, rsem, rsem_here, target, giver):
        def copy():
            return pltpu.make_async_remote_copy(src(), dst(), ssem, rsem, device_id=target, device_id_type=MESH)

        def here():
            return pltpu.make_async_remote_copy(
                src(), recv_dst(), ssem, rsem_here, device_id=giver, device_id_type=MESH
            )

        if recv_when is not None:
            recvs[kind].append((recv_when, here))
        if send_when is not None:
            sends.append((send_when, copy))

            @pl.when(send_when)
            def _():
                copy().start()

    def surface_to(kind, dg, ref, pad, size, ssem, rsem):
        i = (dg + 1) // 2
        message(
            kind, exists(dg, 0), exists(-dg, 0),
            lambda: ref.at[:, giver_rows(dg, pad, size), :],
            lambda: ref.at[:, target_rows(dg, pad, size), :],
            lambda: ref.at[:, target_rows(dg, pad, size), :],
            ssem.at[i], rsem.at[i], rsem.at[i],
            {"sec": s, "gx": g + dg, "gy": h},
            {"sec": s, "gx": g - dg, "gy": h},
        )

    for dg in (-1, 1):
        surface_to("first", dg, cls, extra, deep, cls_send, cls_recv)

    def corner_to(side, dh, keeper, dg):
        size = rows if dg == 0 else deep
        j = dg + 1
        message(
            "first", exists(dg, dh) & (s == keeper), exists(-dg, -dh) & (s == keeper),
            lambda: pack2.at[:, source_rows(dg, size), :],
            lambda: halo2.at[:, target_rows(dg, extra, size), :],
            lambda: halo2.at[:, target_rows(dg, extra, size), :],
            p2_send.at[side * 3 + j], p2_recv.at[side * 3 + j], p2_recv.at[side * 3 + j],
            {"sec": s, "gx": g + dg, "gy": h + dh},
            {"sec": s, "gx": g - dg, "gy": h - dh},
        )

    for side, (dh, keeper) in enumerate(((1, 0), (-1, last))):
        for dg in (-1, 0, 1):
            corner_to(side, dh, keeper, dg)

    def soil_to(dg, t):
        way = (dg + 1) * n_sec
        size = rows if dg == 0 else REACH
        message(
            "soil", exists(dg, 0) if dg else (s != t), exists(-dg, 0) if dg else (s != t),
            lambda: stage3.at[t, :, source_rows(dg, size), :],
            lambda: win3.at[s, :, target_rows(dg, 0, size), :],
            lambda: win3.at[t, :, target_rows(dg, 0, size), :],
            s3_send.at[way + t], s3_recv.at[way + s], s3_recv.at[way + t],
            {"sec": t, "gx": g + dg, "gy": h},
            {"sec": t, "gx": g - dg, "gy": h},
        )

    for dg in (0, -1, 1):
        for t in range(n_sec):
            soil_to(dg, t)

    def soil_edge_to(side, dh, keeper, dg, t):
        way = side * 3 + dg + 1
        size = rows if dg == 0 else REACH
        message(
            "soil", exists(dg, dh) if t == 0 else None, exists(-dg, -dh) & (s == keeper),
            lambda: pack3.at[side, source_rows(dg, size), :],
            lambda: halo3.at[s, target_rows(dg, 0, size), :],
            lambda: halo3.at[t, target_rows(dg, 0, size), :],
            p3_send.at[way], p3_recv.at[way * n_sec + s], p3_recv.at[way * n_sec + t],
            {"sec": keeper, "gx": g + dg, "gy": h + dh},
            {"sec": t, "gx": g - dg, "gy": h - dh},
        )

    for side, (dh, keeper) in enumerate(((1, 0), (-1, last))):
        for dg in (0, -1, 1):
            for t in range(n_sec):
                soil_edge_to(side, dh, keeper, dg, t)

    for dg in (-1, 1):
        surface_to("rest", dg, fld, 0, REACH, fld_send, fld_recv)

    def wait_all(kind):
        for when, copy in recvs[kind]:

            @pl.when(when)
            def _():
                copy().wait_recv()

    soil_slots = 16 * pl.cdiv(soil_embed_ref.shape[0], 16)
    geo_slots = 16 * pl.cdiv(geology_embed_ref.shape[0], 16)
    slots = soil_slots + geo_slots
    table[...] = jnp.zeros(table.shape, F32)
    table[0 : soil_embed_ref.shape[0], :] = soil_embed_ref[...].astype(F32)
    table[soil_slots : soil_slots + geology_embed_ref.shape[0], :] = geology_embed_ref[...].astype(F32)
    embed = table[...].astype(jnp.bfloat16)
    taps[...] = jnp.zeros(taps.shape, F32)
    for i in range(TAPS):
        for j in range(TAPS):
            at = (i * TAPS + j) * slots
            taps[at : at + slots, :] = jnp.dot(embed, conv_ref[i, j], preferred_element_type=F32)
    channels = conv_ref.shape[3]
    depth = TAPS * TAPS * slots
    for k in range(taps.shape[0] // LANES):
        turned = taps[k * LANES : (k + 1) * LANES, :].T
        upper = turned.astype(jnp.bfloat16)
        split[0:channels, k * LANES : (k + 1) * LANES] = upper
        split[channels : 2 * channels, k * LANES : (k + 1) * LANES] = (turned - upper.astype(F32)).astype(
            jnp.bfloat16
        )
    outw_t = outw_ref[...].astype(F32).T.astype(jnp.bfloat16)

    wait_all("first")

    edge_at = jnp.where(s == 0, 0, LANES - margin)

    def edge_mask(shape):
        at = iota(shape, 1)
        return ((s == 0) & (at < margin)) | ((s == last) & (at >= LANES - margin))

    def on_grid(shape, first):
        row = g * rows - offset + first + iota(shape, 0)
        col = h * cols + s * own - margin + iota(shape, 1)
        return (row >= 0) & (row < n_gx * rows) & (col >= 0) & (col < n_gy * cols)

    def unpack(packed, k):
        return pltpu.roll(packed, lax.rem(edge_at - margin * k + LANES, LANES), 1)

    tall = (win_rows + 2 * extra, LANES)
    tall_edge = edge_mask(tall)
    tall_grid = on_grid(tall, -extra)
    for k in range(2):
        merged = jnp.where(tall_edge, unpack(halo2[0], k), cls[k])
        merged = jnp.where(tall_grid, merged, -100.0)
        for j in range(TAPS):
            shifted_cls[j, k] = merged if j == 1 else pltpu.roll(merged, (1 - j) % LANES, 1)

    group = 8

    def make_onehot(it, carry):
        for j in range(TAPS):
            soil_rows = shifted_cls[j, 0, pl.ds(aligned(it * group), group), :]
            geo_rows = shifted_cls[j, 1, pl.ds(aligned(it * group), group), :]
            for k in range(group):
                at = pl.multiple_of(((it * group + k) * TAPS + j) * slots, 16)
                soil_hot = iota((soil_slots, LANES), 0).astype(F32) == soil_rows[k : k + 1]
                geo_hot = iota((geo_slots, LANES), 0).astype(F32) == geo_rows[k : k + 1]
                hot = jnp.concatenate([soil_hot, geo_hot], axis=0)
                onehot[pl.ds(at, slots), :] = jnp.where(hot, 1.0, 0.0).astype(jnp.bfloat16)
        return carry

    lax.fori_loop(0, tall[0] // group, make_onehot, 0)

    def convolve(it, carry):
        r = it * group
        parts = [
            onehot[pl.ds(pl.multiple_of((r + k + extra - 1) * TAPS * slots, 16), depth), :] for k in range(group)
        ]
        both = jnp.dot(split[:, :depth], jnp.concatenate(parts, axis=1), preferred_element_type=F32)
        hidden = jnp.maximum(both[:channels] + both[channels:], 0.0).astype(jnp.bfloat16)
        found = jnp.dot(outw_t, hidden, preferred_element_type=F32)
        stacked = jnp.stack([found[:, k * LANES : (k + 1) * LANES] for k in range(group)], axis=0)
        cond[:, pl.ds(aligned(r), group), :] = jnp.swapaxes(stacked, 0, 1)
        return carry

    lax.fori_loop(0, win_rows // group, convolve, 0)

    flat = (win_rows, LANES)
    grid_mask = on_grid(flat, 0)
    edge = edge_mask(flat)
    row_at = iota(flat, 0)
    lane_at = iota(flat, 1)
    usable = grid_mask & (lane_at > 0) & (lane_at < LANES - 1)
    for l in range(layers):
        cond[l] = jnp.where(usable, jnp.exp(cond[l]), 0.0)

    def north(v):
        return pltpu.roll(v, 1, 0)

    def south(v):
        return pltpu.roll(v, win_rows - 1, 0)

    def east(v):
        return pltpu.roll(v, LANES - 1, 1)

    def west(v):
        return pltpu.roll(v, 1, 1)

    first_row = row_at == 0
    final_row = row_at == win_rows - 1

    def north0(v):
        return jnp.where(first_row, 0.0, north(v))

    def south0(v):
        return jnp.where(final_row, 0.0, south(v))

    wait_all("rest")

    def field(k):
        b, at = (k + 2) // groups, (k + 2) % groups
        merged = jnp.where(edge, unpack(halo2[b, extra : extra + win_rows, :], at), fld[k])
        return jnp.where(grid_mask, merged, 0.0)

    land_w, rough_w, elev_w, rain_w, potential_w, head_w = [field(k) for k in range(6)]
    top_cond = cond[0]
    surf[0] = land_w * (infil_rate * top_cond / (1.0 + top_cond))
    surf[1] = potential_w
    surf[2] = rain_w
    surf[3] = elev_w
    surf[4] = head_w
    total = jnp.zeros(flat, F32)
    for k, move in enumerate((north0, south0, east, west)):
        way = land_w * 0.5 * (rough_w + move(rough_w))
        total = total + way
        surf[5 + k] = way
    surf[9] = total

    wait_all("soil")

    for l in range(layers):
        t, k = l // layers_dev, l % layers_dev
        press = jnp.where(edge, unpack(halo3[t], k), win3[t, k])
        store = jnp.where(edge, unpack(halo3[t], layers_dev + k), win3[t, layers_dev + k])
        press_a[l] = jnp.where(grid_mask, press, 0.0)
        mid = cond[l]
        up = vertical * 0.5 * (mid + cond[l - 1]) if l > 0 else vertical * 0.5 * mid
        down = vertical * 0.5 * (mid + cond[l + 1]) if l < layers - 1 else vertical * 0.5 * mid
        sides = [lateral * 0.5 * (mid + move(mid)) for move in (north0, south0, east, west)]
        diagonal = store + up + down + sides[0] + sides[1] + sides[2] + sides[3]
        inv = jnp.where(grid_mask, 1.0 / jnp.where(grid_mask, diagonal, 1.0), 0.0)
        inverse[l] = inv
        scaled[l] = jnp.where(grid_mask, store, 0.0) * inv
        coef[0, l] = up * inv
        coef[1, l] = down * inv
        coef[2, l] = jnp.where(first_row, 0.0, sides[0] * inv)
        coef[3, l] = jnp.where(final_row, 0.0, sides[1] * inv)
        coef[4, l] = sides[2] * inv
        coef[5, l] = sides[3] * inv

    def sweep(src, dst):
        for l in range(layers):
            mid = src[l]
            new = rhs[l] + coef[2, l] * north(mid) + coef[3, l] * south(mid)
            new = new + coef[4, l] * east(mid) + coef[5, l] * west(mid)
            if l > 0:
                new = new + coef[0, l] * src[l - 1]
            if l < layers - 1:
                new = new + coef[1, l] * src[l + 1]
            dst[l] = new

    def cycle(c, carry):
        top = press_a[0]
        head = surf[4]
        infil = surf[0] * (head - top)
        evap = surf[1] * jax.nn.sigmoid(top)
        level = head + surf[3]
        flux = surf[5] * north0(level) + surf[6] * south0(level)
        flux = flux + surf[7] * east(level) + surf[8] * west(level) - surf[9] * level
        surf[4] = head + (surf[2] - infil + flux)
        for l in range(layers):
            rhs[l] = scaled[l] * press_a[l]
        rhs[0] = rhs[0] + inverse[0] * (infil - evap)

        def pair(i, inner):
            sweep(press_a, press_b)
            sweep(press_b, press_a)
            return inner

        return lax.fori_loop(0, SWEEPS // 2, pair, carry)

    lax.fori_loop(0, CYCLES, cycle, 0)

    mine = pl.ds(aligned(offset), rows)
    low = lane < own
    half = rows // layers_dev
    final_head = surf[4, mine, :]
    head_pack = jnp.where(
        low[:half],
        pltpu.roll(final_head[:half], LANES - margin, 1),
        pltpu.roll(final_head[half:], margin, 1),
    )
    for t in range(n_sec):
        send_out[t, 0:rows, :] = jnp.where(
            low,
            pltpu.roll(press_a[layers_dev * t, mine, :], LANES - margin, 1),
            pltpu.roll(press_a[layers_dev * t + 1, mine, :], margin, 1),
        )
        send_out[t, rows : rows + half, :] = head_pack

    def result_to(t, source):
        return pltpu.make_async_remote_copy(
            send_out.at[t], recv_out.at[source], out_send.at[t], out_recv.at[source],
            device_id={"sec": t, "gx": g, "gy": h}, device_id_type=MESH,
        )

    for t in range(n_sec):

        @pl.when(s != t)
        def _():
            result_to(t, s).start()

    for t in range(n_sec):

        @pl.when(s == t)
        def _():
            recv_out[t] = send_out[t]

    for when, copy in sends:

        @pl.when(when)
        def _():
            copy().wait_send()

    for t in range(n_sec):

        @pl.when(s != t)
        def _():
            result_to(t, t).wait()

    wide = iota((rows + half, LANES), 1) < own
    for m in range(cols // LANES):
        left, right = recv_out[2 * m], recv_out[2 * m + 1]
        even = jnp.where(wide, left, pltpu.roll(right, own, 1))
        odd = jnp.where(wide, pltpu.roll(left, own, 1), right)
        at = slice(m * LANES, (m + 1) * LANES)
        press_out[0, :, at] = even[:rows]
        press_out[1, :, at] = odd[:rows]
        head_out[0:half, at] = even[rows:]
        head_out[half:rows, at] = odd[rows:]


def shards(*args):
    pressure, soil_embed, geology_embed, conv_weight, out_weight = (args[i] for i in (9, 11, 12, 13, 14))
    n_sec, n_gx, n_gy = (lax.axis_size(name) for name in ("sec", "gx", "gy"))
    layers_dev, rows, cols = pressure.shape
    layers = layers_dev * n_sec
    own = cols // n_sec
    margin = (LANES - own) // 2
    assert margin > REACH and layers_dev * own == LANES and 2 * layers_dev * margin == LANES
    assert n_gx >= 2 and rows >= REACH + 8 and layers_dev == 2
    win_rows = rows + 2 * REACH
    channels = conv_weight.shape[3]
    slots = 16 * pl.cdiv(soil_embed.shape[0], 16) + 16 * pl.cdiv(geology_embed.shape[0], 16)
    depth = TAPS * TAPS * slots
    deep = LANES * pl.cdiv(depth, LANES)
    geom = (n_sec, n_gx, n_gy, rows, cols, layers_dev, win_rows)
    vmem = pltpu.VMEM
    dma = pltpu.SemaphoreType.DMA
    bf16 = jnp.bfloat16
    tall = win_rows + 16
    column = (layers, win_rows, LANES)
    scratch = [
        vmem((2, tall, LANES), F32),
        vmem((6, win_rows, LANES), F32),
        vmem((2, rows, LANES), F32),
        vmem((2, tall, LANES), F32),
        vmem((n_sec, 2 * layers_dev, rows, LANES), F32),
        vmem((n_sec, 2 * layers_dev, win_rows, LANES), F32),
        vmem((2, rows, LANES), F32),
        vmem((n_sec, win_rows, LANES), F32),
        vmem((TAPS, 2, tall, LANES), F32),
        vmem((slots, channels), F32),
        vmem((deep, channels), F32),
        vmem((2 * channels, deep), bf16),
        vmem((tall * TAPS * slots, LANES), bf16),
        vmem(column, F32),
        vmem((6,) + column, F32),
        vmem(column, F32),
        vmem(column, F32),
        vmem(column, F32),
        vmem(column, F32),
        vmem(column, F32),
        vmem((10, win_rows, LANES), F32),
        vmem((n_sec, rows + rows // layers_dev, LANES), F32),
        vmem((n_sec, rows + rows // layers_dev, LANES), F32),
        dma((2,)),
        dma((2,)),
        dma((2,)),
        dma((2,)),
        dma((6,)),
        dma((6,)),
        dma((3 * n_sec,)),
        dma((3 * n_sec,)),
        dma((6,)),
        dma((6 * n_sec,)),
        dma((n_sec,)),
        dma((n_sec,)),
    ]
    return pl.pallas_call(
        functools.partial(kernel, geom),
        out_shape=(
            jax.ShapeDtypeStruct(pressure.shape, F32),
            jax.ShapeDtypeStruct((rows, cols), F32),
        ),
        in_specs=[pl.BlockSpec(memory_space=vmem)] * len(args),
        out_specs=(pl.BlockSpec(memory_space=vmem), pl.BlockSpec(memory_space=vmem)),
        scratch_shapes=scratch,
        compiler_params=pltpu.CompilerParams(
            collective_id=0, has_side_effects=True, vmem_limit_bytes=40 * 1024 * 1024
        ),
    )(*args)


def solution(mesh):
    in_specs = (P("gx", "gy"),) * 9 + (P("sec", "gx", "gy"),) * 2 + (P(),) * 4
    out_specs = (P("sec", "gx", "gy"), P("gx", "gy"))
    return jax.shard_map(shards, mesh=mesh, in_specs=in_specs, out_specs=out_specs, check_vma=False)
```

```python
import functools

import jax
import jax.numpy as jnp
from jax import lax
from jax.experimental import pallas as pl
from jax.experimental.pallas import tpu as pltpu
from jax.sharding import PartitionSpec as P

SWEEPS = 4
CYCLES = 4
REACH = SWEEPS * CYCLES
LANES = 128
TAPS = 3

infil_rate = 0.3
lateral = 1.0
vertical = 0.5
F32 = jnp.float32
MESH = pl.DeviceIdType.MESH


def iota(shape, axis):
    return lax.broadcasted_iota(jnp.int32, shape, axis)


def kernel(
    geom,
    soil_ref,
    geology_ref,
    land_ref,
    river_ref,
    elevation_ref,
    roughness_ref,
    rainfall_ref,
    potential_ref,
    head_ref,
    pressure_ref,
    storage_ref,
    soil_embed_ref,
    geology_embed_ref,
    conv_ref,
    outw_ref,
    press_out,
    head_out,
    whole_in,
    real_in,
    soil_in,
    conv_in,
    in_sems,
    cls,
    fld,
    pack2,
    halo2,
    stage3,
    win3,
    pack3,
    halo3,
    shifted_cls,
    table,
    taps,
    split,
    onehot,
    cond,
    coef,
    scaled,
    inverse,
    press_a,
    press_b,
    rhs,
    surf,
    send_out,
    recv_out,
    cls_send,
    cls_recv,
    fld_send,
    fld_recv,
    p2_send,
    p2_recv,
    s3_send,
    s3_recv,
    p3_send,
    p3_recv,
    out_send,
    out_recv,
):
    n_sec, n_gx, n_gy, rows, cols, layers_dev, win_rows = geom
    layers = n_sec * layers_dev
    own = cols // n_sec
    margin = (LANES - own) // 2
    groups = LANES // margin
    s, g, h = (
        jnp.clip(lax.axis_index(name), 0, size - 1) for name, size in (("sec", n_sec), ("gx", n_gx), ("gy", n_gy))
    )
    last = n_sec - 1
    extra = 8
    deep = REACH + extra

    def aligned(value):
        return pl.multiple_of(value, 8)

    offset = REACH * g if n_gx == 2 else REACH

    def exists(dg, dh):
        return (g + dg >= 0) & (g + dg < n_gx) & (h + dh >= 0) & (h + dh < n_gy)

    surface_refs = (
        soil_ref, geology_ref, land_ref, river_ref, elevation_ref, roughness_ref, rainfall_ref, potential_ref, head_ref
    )
    surface_in = [whole_in.at[k] for k in range(4)] + [real_in.at[k] for k in range(5)]
    soil_parts = [soil_in.at[pl.ds(0, layers_dev)], soil_in.at[pl.ds(layers_dev, layers_dev)]]
    loads = [
        pltpu.make_async_copy(src, dst, in_sems.at[k])
        for k, (src, dst) in enumerate(
            zip(
                (*surface_refs, pressure_ref, storage_ref, conv_ref),
                (*surface_in, *soil_parts, conv_in),
            )
        )
    ]
    for load in loads:
        load.start()

    barrier = pltpu.get_barrier_semaphore()
    count = jnp.int32(0)
    for dg in (-1, 0, 1):
        for dh in (-1, 0, 1):
            for t in range(n_sec):
                met = exists(dg, dh)
                if dh == 0 and dg == 0:
                    met = met & (s != t)
                if dh == 1 and t != 0:
                    met = met & (s == last)
                if dh == -1 and t != last:
                    met = met & (s == 0)

                @pl.when(met)
                def _():
                    pl.semaphore_signal(
                        barrier, inc=1, device_id={"sec": t, "gx": g + dg, "gy": h + dh}, device_id_type=MESH
                    )

                count = count + met.astype(jnp.int32)

    for load in loads[:9]:
        load.wait()
    lane = iota((rows, LANES), 1)
    turn = lax.rem(margin - own * s + cols, cols)

    def window_of(values):
        return pltpu.roll(values, turn, 1)[:, :LANES]

    land = whole_in[2].astype(F32)
    rough = land * (1.0 + whole_in[3].astype(F32)) * real_in[1]
    classes = [whole_in[0].astype(F32), whole_in[1].astype(F32)]
    fields = [
        land,
        rough,
        real_in[0],
        land * real_in[2],
        land * real_in[3],
        real_in[4],
    ]
    windows = [window_of(v) for v in classes + fields]
    for k in range(2):
        cls[k, pl.ds(aligned(offset + extra), rows), :] = windows[k]
    for k in range(6):
        fld[k, pl.ds(aligned(offset), rows), :] = windows[2 + k]
    base = jnp.where(s == 0, 0, LANES - margin)
    for b in range(2):
        packed = jnp.zeros((rows, LANES), F32)
        for k in range(groups):
            moved = pltpu.roll(windows[b * groups + k], lax.rem(margin * k - base + LANES, LANES), 1)
            packed = jnp.where((lane >= margin * k) & (lane < margin * (k + 1)), moved, packed)
        pack2[b] = packed

    pl.semaphore_wait(barrier, count)

    def source_rows(dg, size):
        return pl.ds(rows - size if dg == 1 else 0, size)

    def target_rows(dg, pad, size):
        if dg == 0:
            return pl.ds(aligned(offset + pad), size)
        if dg == 1:
            return pl.ds(REACH + pad - size, size)
        return pl.ds((0 if n_gx == 2 else REACH) + rows + pad, size)

    def giver_rows(dg, pad, size):
        if dg == 1:
            return pl.ds((0 if n_gx == 2 else REACH) + pad + rows - size, size)
        return pl.ds(REACH + pad, size)

    sends = []
    recvs = {"first": [], "soil": [], "rest": []}

    def message(kind, send_when, recv_when, src, dst, recv_dst, ssem, rsem, rsem_here, target, giver):
        def copy():
            return pltpu.make_async_remote_copy(src(), dst(), ssem, rsem, device_id=target, device_id_type=MESH)

        def here():
            return pltpu.make_async_remote_copy(
                src(), recv_dst(), ssem, rsem_here, device_id=giver, device_id_type=MESH
            )

        if recv_when is not None:
            recvs[kind].append((recv_when, here))
        if send_when is not None:
            sends.append((send_when, copy))

            @pl.when(send_when)
            def _():
                copy().start()

    def surface_to(kind, dg, ref, pad, size, ssem, rsem):
        i = (dg + 1) // 2
        message(
            kind, exists(dg, 0), exists(-dg, 0),
            lambda: ref.at[:, giver_rows(dg, pad, size), :],
            lambda: ref.at[:, target_rows(dg, pad, size), :],
            lambda: ref.at[:, target_rows(dg, pad, size), :],
            ssem.at[i], rsem.at[i], rsem.at[i],
            {"sec": s, "gx": g + dg, "gy": h},
            {"sec": s, "gx": g - dg, "gy": h},
        )

    for dg in (-1, 1):
        surface_to("first", dg, cls, extra, deep, cls_send, cls_recv)

    def corner_to(side, dh, keeper, dg):
        size = rows if dg == 0 else deep
        j = dg + 1
        message(
            "first", exists(dg, dh) & (s == keeper), exists(-dg, -dh) & (s == keeper),
            lambda: pack2.at[:, source_rows(dg, size), :],
            lambda: halo2.at[:, target_rows(dg, extra, size), :],
            lambda: halo2.at[:, target_rows(dg, extra, size), :],
            p2_send.at[side * 3 + j], p2_recv.at[side * 3 + j], p2_recv.at[side * 3 + j],
            {"sec": s, "gx": g + dg, "gy": h + dh},
            {"sec": s, "gx": g - dg, "gy": h - dh},
        )

    for side, (dh, keeper) in enumerate(((1, 0), (-1, last))):
        for dg in (-1, 0, 1):
            corner_to(side, dh, keeper, dg)

    loads[9].wait()
    loads[10].wait()
    soil_blocks = [soil_in[k] for k in range(2 * layers_dev)]
    n_blocks = len(soil_blocks)
    for t in range(n_sec):
        for k in range(n_blocks):
            stage3[t, k] = pltpu.roll(soil_blocks[k], (margin - own * t) % cols, 1)[:, :LANES]
    for side, (t, edge) in enumerate(((0, 0), (last, LANES - margin))):
        packed = jnp.zeros((rows, LANES), F32)
        for k in range(n_blocks):
            moved = pltpu.roll(stage3[t, k], (margin * k - edge) % LANES, 1)
            packed = jnp.where((lane >= margin * k) & (lane < margin * (k + 1)), moved, packed)
        pack3[side] = packed
    for t in range(n_sec):

        @pl.when(s == t)
        def _():
            for k in range(n_blocks):
                win3[t, k, pl.ds(aligned(offset), rows), :] = stage3[t, k]


    def soil_to(dg, t):
        way = (dg + 1) * n_sec
        size = rows if dg == 0 else REACH
        message(
            "soil", exists(dg, 0) if dg else (s != t), exists(-dg, 0) if dg else (s != t),
            lambda: stage3.at[t, :, source_rows(dg, size), :],
            lambda: win3.at[s, :, target_rows(dg, 0, size), :],
            lambda: win3.at[t, :, target_rows(dg, 0, size), :],
            s3_send.at[way + t], s3_recv.at[way + s], s3_recv.at[way + t],
            {"sec": t, "gx": g + dg, "gy": h},
            {"sec": t, "gx": g - dg, "gy": h},
        )

    for dg in (0, -1, 1):
        for t in range(n_sec):
            soil_to(dg, t)

    def soil_edge_to(side, dh, keeper, dg, t):
        way = side * 3 + dg + 1
        size = rows if dg == 0 else REACH
        message(
            "soil", exists(dg, dh) if t == 0 else None, exists(-dg, -dh) & (s == keeper),
            lambda: pack3.at[side, source_rows(dg, size), :],
            lambda: halo3.at[s, target_rows(dg, 0, size), :],
            lambda: halo3.at[t, target_rows(dg, 0, size), :],
            p3_send.at[way], p3_recv.at[way * n_sec + s], p3_recv.at[way * n_sec + t],
            {"sec": keeper, "gx": g + dg, "gy": h + dh},
            {"sec": t, "gx": g - dg, "gy": h - dh},
        )

    for side, (dh, keeper) in enumerate(((1, 0), (-1, last))):
        for dg in (0, -1, 1):
            for t in range(n_sec):
                soil_edge_to(side, dh, keeper, dg, t)

    for dg in (-1, 1):
        surface_to("rest", dg, fld, 0, REACH, fld_send, fld_recv)

    def wait_all(kind):
        for when, copy in recvs[kind]:

            @pl.when(when)
            def _():
                copy().wait_recv()

    soil_slots = 16 * pl.cdiv(soil_embed_ref.shape[0], 16)
    geo_slots = 16 * pl.cdiv(geology_embed_ref.shape[0], 16)
    slots = soil_slots + geo_slots
    table[...] = jnp.zeros(table.shape, F32)
    table[0 : soil_embed_ref.shape[0], :] = soil_embed_ref[...].astype(F32)
    table[soil_slots : soil_slots + geology_embed_ref.shape[0], :] = geology_embed_ref[...].astype(F32)
    embed = table[...].astype(jnp.bfloat16)
    loads[11].wait()
    taps[...] = jnp.zeros(taps.shape, F32)
    for i in range(TAPS):
        for j in range(TAPS):
            at = (i * TAPS + j) * slots
            taps[at : at + slots, :] = jnp.dot(embed, conv_in[i, j], preferred_element_type=F32)
    channels = conv_ref.shape[3]
    depth = TAPS * TAPS * slots
    for k in range(taps.shape[0] // LANES):
        turned = taps[k * LANES : (k + 1) * LANES, :].T
        upper = turned.astype(jnp.bfloat16)
        split[0:channels, k * LANES : (k + 1) * LANES] = upper
        split[channels : 2 * channels, k * LANES : (k + 1) * LANES] = (turned - upper.astype(F32)).astype(
            jnp.bfloat16
        )
    outw_t = outw_ref[...]

    wait_all("first")

    edge_at = jnp.where(s == 0, 0, LANES - margin)

    def edge_mask(shape):
        at = iota(shape, 1)
        return ((s == 0) & (at < margin)) | ((s == last) & (at >= LANES - margin))

    def on_grid(shape, first):
        row = g * rows - offset + first + iota(shape, 0)
        col = h * cols + s * own - margin + iota(shape, 1)
        return (row >= 0) & (row < n_gx * rows) & (col >= 0) & (col < n_gy * cols)

    def unpack(packed, k):
        return pltpu.roll(packed, lax.rem(edge_at - margin * k + LANES, LANES), 1)

    tall = (win_rows + 2 * extra, LANES)
    tall_edge = edge_mask(tall)
    tall_grid = on_grid(tall, -extra)
    for k in range(2):
        merged = jnp.where(tall_edge, unpack(halo2[0], k), cls[k])
        merged = jnp.where(tall_grid, merged, -100.0)
        for j in range(TAPS):
            shifted_cls[j, k] = merged if j == 1 else pltpu.roll(merged, (1 - j) % LANES, 1)

    group = 8

    def make_onehot(it, carry):
        for j in range(TAPS):
            soil_rows = shifted_cls[j, 0, pl.ds(aligned(it * group), group), :]
            geo_rows = shifted_cls[j, 1, pl.ds(aligned(it * group), group), :]
            for k in range(group):
                at = pl.multiple_of(((it * group + k) * TAPS + j) * slots, 16)
                soil_hot = iota((soil_slots, LANES), 0).astype(F32) == soil_rows[k : k + 1]
                geo_hot = iota((geo_slots, LANES), 0).astype(F32) == geo_rows[k : k + 1]
                hot = jnp.concatenate([soil_hot, geo_hot], axis=0)
                onehot[pl.ds(at, slots), :] = jnp.where(hot, 1.0, 0.0).astype(jnp.bfloat16)
        return carry

    lax.fori_loop(0, tall[0] // group, make_onehot, 0)

    def convolve(it, carry):
        r = it * group
        parts = [
            onehot[pl.ds(pl.multiple_of((r + k + extra - 1) * TAPS * slots, 16), depth), :] for k in range(group)
        ]
        both = jnp.dot(split[:, :depth], jnp.concatenate(parts, axis=1), preferred_element_type=F32)
        hidden = jnp.maximum(both[:channels] + both[channels:], 0.0).astype(jnp.bfloat16)
        found = jnp.dot(outw_t, hidden, preferred_element_type=F32)
        stacked = jnp.stack([found[:, k * LANES : (k + 1) * LANES] for k in range(group)], axis=0)
        cond[:, pl.ds(aligned(r), group), :] = jnp.swapaxes(stacked, 0, 1)
        return carry

    lax.fori_loop(0, win_rows // group, convolve, 0)

    flat = (win_rows, LANES)
    grid_mask = on_grid(flat, 0)
    edge = edge_mask(flat)
    row_at = iota(flat, 0)
    lane_at = iota(flat, 1)
    usable = grid_mask & (lane_at > 0) & (lane_at < LANES - 1)
    for l in range(layers):
        cond[l] = jnp.where(usable, jnp.exp(cond[l]), 0.0)

    def north(v):
        return pltpu.roll(v, 1, 0)

    def south(v):
        return pltpu.roll(v, win_rows - 1, 0)

    def east(v):
        return pltpu.roll(v, LANES - 1, 1)

    def west(v):
        return pltpu.roll(v, 1, 1)

    first_row = row_at == 0
    final_row = row_at == win_rows - 1

    def north0(v):
        return jnp.where(first_row, 0.0, north(v))

    def south0(v):
        return jnp.where(final_row, 0.0, south(v))

    wait_all("rest")

    def field(k):
        b, at = (k + 2) // groups, (k + 2) % groups
        merged = jnp.where(edge, unpack(halo2[b, extra : extra + win_rows, :], at), fld[k])
        return jnp.where(grid_mask, merged, 0.0)

    land_w, rough_w, elev_w, rain_w, potential_w, head_w = [field(k) for k in range(6)]
    top_cond = cond[0]
    surf[0] = land_w * (infil_rate * top_cond / (1.0 + top_cond))
    surf[1] = potential_w
    surf[2] = rain_w
    surf[3] = elev_w
    surf[4] = head_w
    total = jnp.zeros(flat, F32)
    for k, move in enumerate((north0, south0, east, west)):
        way = land_w * 0.5 * (rough_w + move(rough_w))
        total = total + way
        surf[5 + k] = way
    surf[9] = total

    wait_all("soil")

    for l in range(layers):
        t, k = l // layers_dev, l % layers_dev
        press = jnp.where(edge, unpack(halo3[t], k), win3[t, k])
        store = jnp.where(edge, unpack(halo3[t], layers_dev + k), win3[t, layers_dev + k])
        press_a[l] = jnp.where(grid_mask, press, 0.0)
        mid = cond[l]
        up = vertical * 0.5 * (mid + cond[l - 1]) if l > 0 else vertical * 0.5 * mid
        down = vertical * 0.5 * (mid + cond[l + 1]) if l < layers - 1 else vertical * 0.5 * mid
        sides = [lateral * 0.5 * (mid + move(mid)) for move in (north0, south0, east, west)]
        diagonal = store + up + down + sides[0] + sides[1] + sides[2] + sides[3]
        inv = jnp.where(grid_mask, 1.0 / jnp.where(grid_mask, diagonal, 1.0), 0.0)
        inverse[l] = inv
        scaled[l] = jnp.where(grid_mask, store, 0.0) * inv
        coef[0, l] = up * inv
        coef[1, l] = down * inv
        coef[2, l] = jnp.where(first_row, 0.0, sides[0] * inv)
        coef[3, l] = jnp.where(final_row, 0.0, sides[1] * inv)
        coef[4, l] = sides[2] * inv
        coef[5, l] = sides[3] * inv

    def sweep(src, dst):
        for l in range(layers):
            mid = src[l]
            new = rhs[l] + coef[2, l] * north(mid) + coef[3, l] * south(mid)
            new = new + coef[4, l] * east(mid) + coef[5, l] * west(mid)
            if l > 0:
                new = new + coef[0, l] * src[l - 1]
            if l < layers - 1:
                new = new + coef[1, l] * src[l + 1]
            dst[l] = new

    def cycle(c, carry):
        top = press_a[0]
        head = surf[4]
        infil = surf[0] * (head - top)
        evap = surf[1] * jax.nn.sigmoid(top)
        level = head + surf[3]
        flux = surf[5] * north0(level) + surf[6] * south0(level)
        flux = flux + surf[7] * east(level) + surf[8] * west(level) - surf[9] * level
        surf[4] = head + (surf[2] - infil + flux)
        for l in range(layers):
            rhs[l] = scaled[l] * press_a[l]
        rhs[0] = rhs[0] + inverse[0] * (infil - evap)

        def pair(i, inner):
            sweep(press_a, press_b)
            sweep(press_b, press_a)
            return inner

        return lax.fori_loop(0, SWEEPS // 2, pair, carry)

    lax.fori_loop(0, CYCLES, cycle, 0)

    mine = pl.ds(aligned(offset), rows)
    low = lane < own
    half = rows // layers_dev
    final_head = surf[4, mine, :]
    head_pack = jnp.where(
        low[:half],
        pltpu.roll(final_head[:half], LANES - margin, 1),
        pltpu.roll(final_head[half:], margin, 1),
    )
    for t in range(n_sec):
        send_out[t, 0:rows, :] = jnp.where(
            low,
            pltpu.roll(press_a[layers_dev * t, mine, :], LANES - margin, 1),
            pltpu.roll(press_a[layers_dev * t + 1, mine, :], margin, 1),
        )
        send_out[t, rows : rows + half, :] = head_pack

    def result_to(t, source):
        return pltpu.make_async_remote_copy(
            send_out.at[t], recv_out.at[source], out_send.at[t], out_recv.at[source],
            device_id={"sec": t, "gx": g, "gy": h}, device_id_type=MESH,
        )

    for t in range(n_sec):

        @pl.when(s != t)
        def _():
            result_to(t, s).start()

    for t in range(n_sec):

        @pl.when(s == t)
        def _():
            recv_out[t] = send_out[t]

    for when, copy in sends:

        @pl.when(when)
        def _():
            copy().wait_send()

    for t in range(n_sec):

        @pl.when(s != t)
        def _():
            result_to(t, t).wait()

    wide = iota((rows + half, LANES), 1) < own
    for m in range(cols // LANES):
        left, right = recv_out[2 * m], recv_out[2 * m + 1]
        even = jnp.where(wide, left, pltpu.roll(right, own, 1))
        odd = jnp.where(wide, pltpu.roll(left, own, 1), right)
        at = slice(m * LANES, (m + 1) * LANES)
        press_out[0, :, at] = even[:rows]
        press_out[1, :, at] = odd[:rows]
        head_out[0:half, at] = even[rows:]
        head_out[half:rows, at] = odd[rows:]


def shards(*args):
    pressure, soil_embed, geology_embed, conv_weight, out_weight = (args[i] for i in (9, 11, 12, 13, 14))
    n_sec, n_gx, n_gy = (lax.axis_size(name) for name in ("sec", "gx", "gy"))
    layers_dev, rows, cols = pressure.shape
    layers = layers_dev * n_sec
    own = cols // n_sec
    margin = (LANES - own) // 2
    assert margin > REACH and layers_dev * own == LANES and 2 * layers_dev * margin == LANES
    assert n_gx >= 2 and rows >= REACH + 8 and layers_dev == 2
    win_rows = rows + (REACH if n_gx == 2 else 2 * REACH)
    channels = conv_weight.shape[3]
    slots = 16 * pl.cdiv(soil_embed.shape[0], 16) + 16 * pl.cdiv(geology_embed.shape[0], 16)
    depth = TAPS * TAPS * slots
    deep = LANES * pl.cdiv(depth, LANES)
    geom = (n_sec, n_gx, n_gy, rows, cols, layers_dev, win_rows)
    vmem = pltpu.VMEM
    dma = pltpu.SemaphoreType.DMA
    bf16 = jnp.bfloat16
    tall = win_rows + 16
    column = (layers, win_rows, LANES)
    scratch = [
        vmem((4, rows, cols), jnp.int32),
        vmem((5, rows, cols), F32),
        vmem((2 * layers_dev, rows, cols), F32),
        vmem(conv_weight.shape, bf16),
        dma((12,)),
        vmem((2, tall, LANES), F32),
        vmem((6, win_rows, LANES), F32),
        vmem((2, rows, LANES), F32),
        vmem((2, tall, LANES), F32),
        vmem((n_sec, 2 * layers_dev, rows, LANES), F32),
        vmem((n_sec, 2 * layers_dev, win_rows, LANES), F32),
        vmem((2, rows, LANES), F32),
        vmem((n_sec, win_rows, LANES), F32),
        vmem((TAPS, 2, tall, LANES), F32),
        vmem((slots, channels), F32),
        vmem((deep, channels), F32),
        vmem((2 * channels, deep), bf16),
        vmem((tall * TAPS * slots, LANES), bf16),
        vmem(column, F32),
        vmem((6,) + column, F32),
        vmem(column, F32),
        vmem(column, F32),
        vmem(column, F32),
        vmem(column, F32),
        vmem(column, F32),
        vmem((10, win_rows, LANES), F32),
        vmem((n_sec, rows + rows // layers_dev, LANES), F32),
        vmem((n_sec, rows + rows // layers_dev, LANES), F32),
        dma((2,)),
        dma((2,)),
        dma((2,)),
        dma((2,)),
        dma((6,)),
        dma((6,)),
        dma((3 * n_sec,)),
        dma((3 * n_sec,)),
        dma((6,)),
        dma((6 * n_sec,)),
        dma((n_sec,)),
        dma((n_sec,)),
    ]
    return pl.pallas_call(
        functools.partial(kernel, geom),
        out_shape=(
            jax.ShapeDtypeStruct(pressure.shape, F32),
            jax.ShapeDtypeStruct((rows, cols), F32),
        ),
        in_specs=[pl.BlockSpec(memory_space=vmem if k in (11, 12, 14) else pl.ANY) for k in range(len(args))],
        out_specs=(pl.BlockSpec(memory_space=vmem), pl.BlockSpec(memory_space=vmem)),
        scratch_shapes=scratch,
        compiler_params=pltpu.CompilerParams(
            collective_id=0, has_side_effects=True, vmem_limit_bytes=62 * 1024 * 1024
        ),
    )(*args[:14], out_weight.T)


def solution(mesh):
    in_specs = (P("gx", "gy"),) * 9 + (P("sec", "gx", "gy"),) * 2 + (P(),) * 4
    out_specs = (P("sec", "gx", "gy"), P("gx", "gy"))
    return jax.shard_map(shards, mesh=mesh, in_specs=in_specs, out_specs=out_specs, check_vma=False)
```

```python
import functools

import jax
import jax.numpy as jnp
from jax import lax
from jax.experimental import pallas as pl
from jax.experimental.pallas import tpu as pltpu
from jax.sharding import PartitionSpec as P

SWEEPS = 4
CYCLES = 4
REACH = SWEEPS * CYCLES
LANES = 128
TAPS = 3

infil_rate = 0.3
lateral = 1.0
vertical = 0.5
F32 = jnp.float32
MESH = pl.DeviceIdType.MESH


def iota(shape, axis):
    return lax.broadcasted_iota(jnp.int32, shape, axis)


def kernel(
    geom,
    soil_ref,
    geology_ref,
    land_ref,
    river_ref,
    elevation_ref,
    roughness_ref,
    rainfall_ref,
    potential_ref,
    head_ref,
    pressure_ref,
    storage_ref,
    soil_embed_ref,
    geology_embed_ref,
    conv_ref,
    outw_ref,
    press_out,
    head_out,
    whole_in,
    real_in,
    soil_in,
    conv_in,
    in_sems,
    cls,
    fld,
    pack2,
    halo2,
    stage3,
    win3,
    pack3,
    halo3,
    shifted_cls,
    table,
    taps,
    split,
    onehot,
    cond,
    coef,
    scaled,
    inverse,
    press_a,
    press_b,
    rhs,
    surf,
    send_out,
    recv_out,
    cls_send,
    cls_recv,
    fld_send,
    fld_recv,
    p2_send,
    p2_recv,
    s3_send,
    s3_recv,
    p3_send,
    p3_recv,
    out_send,
    out_recv,
):
    n_sec, n_gx, n_gy, rows, cols, layers_dev, win_rows = geom
    layers = n_sec * layers_dev
    own = cols // n_sec
    margin = (LANES - own) // 2
    groups = LANES // margin
    keep = own + 2 * REACH
    low_lane = margin - REACH
    piece = LANES - keep
    s, g, h = (
        jnp.clip(lax.axis_index(name), 0, size - 1) for name, size in (("sec", n_sec), ("gx", n_gx), ("gy", n_gy))
    )
    last = n_sec - 1
    extra = 8
    deep = REACH + extra

    def aligned(value):
        return pl.multiple_of(value, 8)

    offset = REACH * g if n_gx == 2 else REACH

    def exists(dg, dh):
        return (g + dg >= 0) & (g + dg < n_gx) & (h + dh >= 0) & (h + dh < n_gy)

    surface_refs = (
        soil_ref, geology_ref, land_ref, river_ref, elevation_ref, roughness_ref, rainfall_ref, potential_ref, head_ref
    )
    surface_in = [whole_in.at[k] for k in range(4)] + [real_in.at[k] for k in range(5)]
    soil_parts = [soil_in.at[pl.ds(0, layers_dev)], soil_in.at[pl.ds(layers_dev, layers_dev)]]
    loads = [
        pltpu.make_async_copy(src, dst, in_sems.at[k])
        for k, (src, dst) in enumerate(
            zip(
                (*surface_refs, pressure_ref, storage_ref, conv_ref),
                (*surface_in, *soil_parts, conv_in),
            )
        )
    ]
    for load in loads:
        load.start()

    barrier = pltpu.get_barrier_semaphore()
    count = jnp.int32(0)
    for dg in (-1, 0, 1):
        for dh in (-1, 0, 1):
            for t in range(n_sec):
                met = exists(dg, dh)
                if dh == 0 and dg == 0:
                    met = met & (s != t)
                if dh == 1 and t != 0:
                    met = met & (s == last)
                if dh == -1 and t != last:
                    met = met & (s == 0)

                @pl.when(met)
                def _():
                    pl.semaphore_signal(
                        barrier, inc=1, device_id={"sec": t, "gx": g + dg, "gy": h + dh}, device_id_type=MESH
                    )

                count = count + met.astype(jnp.int32)

    for load in loads[:9]:
        load.wait()
    lane = iota((rows, LANES), 1)
    turn = lax.rem(margin - own * s + cols, cols)

    def window_of(values):
        return pltpu.roll(values, turn, 1)[:, :LANES]

    land = whole_in[2].astype(F32)
    rough = land * (1.0 + whole_in[3].astype(F32)) * real_in[1]
    classes = [whole_in[0].astype(F32), whole_in[1].astype(F32)]
    fields = [
        land,
        rough,
        real_in[0],
        land * real_in[2],
        land * real_in[3],
        real_in[4],
    ]
    windows = [window_of(v) for v in classes + fields]
    for k in range(2):
        cls[k, pl.ds(aligned(offset + extra), rows), :] = windows[k]
    for k in range(6):
        fld[k, pl.ds(aligned(offset), rows), :] = windows[2 + k]
    base = jnp.where(s == 0, 0, LANES - margin)
    for b in range(2):
        packed = jnp.zeros((rows, LANES), F32)
        for k in range(groups):
            moved = pltpu.roll(windows[b * groups + k], lax.rem(margin * k - base + LANES, LANES), 1)
            packed = jnp.where((lane >= margin * k) & (lane < margin * (k + 1)), moved, packed)
        pack2[b] = packed

    pl.semaphore_wait(barrier, count)

    def source_rows(dg, size):
        return pl.ds(rows - size if dg == 1 else 0, size)

    def target_rows(dg, pad, size):
        if dg == 0:
            return pl.ds(aligned(offset + pad), size)
        if dg == 1:
            return pl.ds(REACH + pad - size, size)
        return pl.ds((0 if n_gx == 2 else REACH) + rows + pad, size)

    def giver_rows(dg, pad, size):
        if dg == 1:
            return pl.ds((0 if n_gx == 2 else REACH) + pad + rows - size, size)
        return pl.ds(REACH + pad, size)

    sends = []
    recvs = {"first": [], "soil": [], "rest": []}

    def message(kind, send_when, recv_when, src, dst, recv_dst, ssem, rsem, rsem_here, target, giver):
        def copy():
            return pltpu.make_async_remote_copy(src(), dst(), ssem, rsem, device_id=target, device_id_type=MESH)

        def here():
            return pltpu.make_async_remote_copy(
                src(), recv_dst(), ssem, rsem_here, device_id=giver, device_id_type=MESH
            )

        if recv_when is not None:
            recvs[kind].append((recv_when, here))
        if send_when is not None:
            sends.append((send_when, copy))

            @pl.when(send_when)
            def _():
                copy().start()

    def surface_to(kind, dg, ref, pad, size, ssem, rsem):
        i = (dg + 1) // 2
        message(
            kind, exists(dg, 0), exists(-dg, 0),
            lambda: ref.at[:, giver_rows(dg, pad, size), :],
            lambda: ref.at[:, target_rows(dg, pad, size), :],
            lambda: ref.at[:, target_rows(dg, pad, size), :],
            ssem.at[i], rsem.at[i], rsem.at[i],
            {"sec": s, "gx": g + dg, "gy": h},
            {"sec": s, "gx": g - dg, "gy": h},
        )

    for dg in (-1, 1):
        surface_to("first", dg, cls, extra, deep, cls_send, cls_recv)

    def corner_to(side, dh, keeper, dg):
        size = rows if dg == 0 else deep
        j = dg + 1
        message(
            "first", exists(dg, dh) & (s == keeper), exists(-dg, -dh) & (s == keeper),
            lambda: pack2.at[:, source_rows(dg, size), :],
            lambda: halo2.at[:, target_rows(dg, extra, size), :],
            lambda: halo2.at[:, target_rows(dg, extra, size), :],
            p2_send.at[side * 3 + j], p2_recv.at[side * 3 + j], p2_recv.at[side * 3 + j],
            {"sec": s, "gx": g + dg, "gy": h + dh},
            {"sec": s, "gx": g - dg, "gy": h - dh},
        )

    for side, (dh, keeper) in enumerate(((1, 0), (-1, last))):
        for dg in (-1, 0, 1):
            corner_to(side, dh, keeper, dg)

    for dg in (-1, 1):
        surface_to("rest", dg, fld, 0, REACH, fld_send, fld_recv)

    loads[9].wait()
    loads[10].wait()
    soil_blocks = [soil_in[k] for k in range(2 * layers_dev)]
    n_blocks = len(soil_blocks)
    sides3 = {0: (0, 0), last: (1, LANES - margin)}
    for t in range(n_sec):
        blocks = [pltpu.roll(v, (margin - own * t) % cols, 1)[:, :LANES] for v in soil_blocks]
        for j in range(n_blocks - 1):
            moved = pltpu.roll(blocks[-1], (keep - piece * j) % LANES, 1)
            stage3[t, j] = jnp.where((lane >= low_lane) & (lane < low_lane + keep), blocks[j], moved)
        if t in sides3:
            side, edge = sides3[t]
            packed = jnp.zeros((rows, LANES), F32)
            for k in range(n_blocks):
                moved = pltpu.roll(blocks[k], (margin * k - edge) % LANES, 1)
                packed = jnp.where((lane >= margin * k) & (lane < margin * (k + 1)), moved, packed)
            pack3[side] = packed
    for t in range(n_sec):

        @pl.when(s == t)
        def _():
            for j in range(n_blocks - 1):
                win3[t, j, pl.ds(aligned(offset), rows), :] = stage3[t, j]

    def soil_to(dg, t):
        way = (dg + 1) * n_sec
        size = rows if dg == 0 else REACH
        message(
            "soil", exists(dg, 0) if dg else (s != t), exists(-dg, 0) if dg else (s != t),
            lambda: stage3.at[t, :, source_rows(dg, size), :],
            lambda: win3.at[s, :, target_rows(dg, 0, size), :],
            lambda: win3.at[t, :, target_rows(dg, 0, size), :],
            s3_send.at[way + t], s3_recv.at[way + s], s3_recv.at[way + t],
            {"sec": t, "gx": g + dg, "gy": h},
            {"sec": t, "gx": g - dg, "gy": h},
        )

    for dg in (0, -1, 1):
        for t in range(n_sec):
            soil_to(dg, t)

    def soil_edge_to(side, dh, keeper, dg, t):
        way = side * 3 + dg + 1
        size = rows if dg == 0 else REACH
        message(
            "soil", exists(dg, dh) if t == 0 else None, exists(-dg, -dh) & (s == keeper),
            lambda: pack3.at[side, source_rows(dg, size), :],
            lambda: halo3.at[s, target_rows(dg, 0, size), :],
            lambda: halo3.at[t, target_rows(dg, 0, size), :],
            p3_send.at[way], p3_recv.at[way * n_sec + s], p3_recv.at[way * n_sec + t],
            {"sec": keeper, "gx": g + dg, "gy": h + dh},
            {"sec": t, "gx": g - dg, "gy": h - dh},
        )

    for side, (dh, keeper) in enumerate(((1, 0), (-1, last))):
        for dg in (0, -1, 1):
            for t in range(n_sec):
                soil_edge_to(side, dh, keeper, dg, t)

    def wait_all(kind):
        for when, copy in recvs[kind]:

            @pl.when(when)
            def _():
                copy().wait_recv()

    soil_slots = 16 * pl.cdiv(soil_embed_ref.shape[0], 16)
    geo_slots = 16 * pl.cdiv(geology_embed_ref.shape[0], 16)
    slots = soil_slots + geo_slots
    table[...] = jnp.zeros(table.shape, F32)
    table[0 : soil_embed_ref.shape[0], :] = soil_embed_ref[...].astype(F32)
    table[soil_slots : soil_slots + geology_embed_ref.shape[0], :] = geology_embed_ref[...].astype(F32)
    embed = table[...].astype(jnp.bfloat16)
    loads[11].wait()
    taps[...] = jnp.zeros(taps.shape, F32)
    for i in range(TAPS):
        for j in range(TAPS):
            at = (i * TAPS + j) * slots
            taps[at : at + slots, :] = jnp.dot(embed, conv_in[i, j], preferred_element_type=F32)
    channels = conv_ref.shape[3]
    depth = TAPS * TAPS * slots
    for k in range(taps.shape[0] // LANES):
        turned = taps[k * LANES : (k + 1) * LANES, :].T
        upper = turned.astype(jnp.bfloat16)
        split[0:channels, k * LANES : (k + 1) * LANES] = upper
        split[channels : 2 * channels, k * LANES : (k + 1) * LANES] = (turned - upper.astype(F32)).astype(
            jnp.bfloat16
        )
    outw_t = outw_ref[...]

    wait_all("first")

    edge_at = jnp.where(s == 0, 0, LANES - margin)

    def edge_mask(shape):
        at = iota(shape, 1)
        return ((s == 0) & (at < margin)) | ((s == last) & (at >= LANES - margin))

    def on_grid(shape, first):
        row = g * rows - offset + first + iota(shape, 0)
        col = h * cols + s * own - margin + iota(shape, 1)
        return (row >= 0) & (row < n_gx * rows) & (col >= 0) & (col < n_gy * cols)

    def unpack(packed, k):
        return pltpu.roll(packed, lax.rem(edge_at - margin * k + LANES, LANES), 1)

    tall = (win_rows + 2 * extra, LANES)
    tall_edge = edge_mask(tall)
    tall_grid = on_grid(tall, -extra)
    for k in range(2):
        merged = jnp.where(tall_edge, unpack(halo2[0], k), cls[k])
        merged = jnp.where(tall_grid, merged, -100.0)
        for j in range(TAPS):
            shifted_cls[j, k] = merged if j == 1 else pltpu.roll(merged, (1 - j) % LANES, 1)

    group = 8

    def make_onehot(it, carry):
        for j in range(TAPS):
            soil_rows = shifted_cls[j, 0, pl.ds(aligned(it * group), group), :]
            geo_rows = shifted_cls[j, 1, pl.ds(aligned(it * group), group), :]
            for k in range(group):
                at = pl.multiple_of(((it * group + k) * TAPS + j) * slots, 16)
                soil_hot = iota((soil_slots, LANES), 0).astype(F32) == soil_rows[k : k + 1]
                geo_hot = iota((geo_slots, LANES), 0).astype(F32) == geo_rows[k : k + 1]
                hot = jnp.concatenate([soil_hot, geo_hot], axis=0)
                onehot[pl.ds(at, slots), :] = jnp.where(hot, 1.0, 0.0).astype(jnp.bfloat16)
        return carry

    lax.fori_loop(0, tall[0] // group, make_onehot, 0)

    def convolve(it, carry):
        r = it * group
        parts = [
            onehot[pl.ds(pl.multiple_of((r + k + extra - 1) * TAPS * slots, 16), depth), :] for k in range(group)
        ]
        both = jnp.dot(split[:, :depth], jnp.concatenate(parts, axis=1), preferred_element_type=F32)
        hidden = jnp.maximum(both[:channels] + both[channels:], 0.0).astype(jnp.bfloat16)
        found = jnp.dot(outw_t, hidden, preferred_element_type=F32)
        stacked = jnp.stack([found[:, k * LANES : (k + 1) * LANES] for k in range(group)], axis=0)
        cond[:, pl.ds(aligned(r), group), :] = jnp.swapaxes(stacked, 0, 1)
        return carry

    lax.fori_loop(0, win_rows // group, convolve, 0)

    flat = (win_rows, LANES)
    grid_mask = on_grid(flat, 0)
    edge = edge_mask(flat)
    row_at = iota(flat, 0)
    lane_at = iota(flat, 1)
    usable = grid_mask & (lane_at > 0) & (lane_at < LANES - 1)
    for l in range(layers):
        cond[l] = jnp.where(usable, jnp.exp(cond[l]), 0.0)

    def north(v):
        return pltpu.roll(v, 1, 0)

    def south(v):
        return pltpu.roll(v, win_rows - 1, 0)

    def east(v):
        return pltpu.roll(v, LANES - 1, 1)

    def west(v):
        return pltpu.roll(v, 1, 1)

    first_row = row_at == 0
    final_row = row_at == win_rows - 1

    def north0(v):
        return jnp.where(first_row, 0.0, north(v))

    def south0(v):
        return jnp.where(final_row, 0.0, south(v))

    wait_all("rest")

    def field(k):
        b, at = (k + 2) // groups, (k + 2) % groups
        merged = jnp.where(edge, unpack(halo2[b, extra : extra + win_rows, :], at), fld[k])
        return jnp.where(grid_mask, merged, 0.0)

    land_w, rough_w, elev_w, rain_w, potential_w, head_w = [field(k) for k in range(6)]
    top_cond = cond[0]
    surf[0] = land_w * (infil_rate * top_cond / (1.0 + top_cond))
    surf[1] = potential_w
    surf[2] = rain_w
    surf[3] = elev_w
    surf[4] = head_w
    total = jnp.zeros(flat, F32)
    for k, move in enumerate((north0, south0, east, west)):
        way = land_w * 0.5 * (rough_w + move(rough_w))
        total = total + way
        surf[5 + k] = way
    surf[9] = total

    wait_all("soil")

    soil_mask = grid_mask & (lane_at >= low_lane) & (lane_at < low_lane + keep)

    def soil_block(t, k):
        if k < n_blocks - 1:
            found = win3[t, k]
        else:
            found = pltpu.roll(win3[t, 0], (-keep) % LANES, 1)
            for j in range(1, n_blocks - 1):
                back = pltpu.roll(win3[t, j], (piece * j - keep) % LANES, 1)
                found = jnp.where(lane_at < low_lane + piece * j, found, back)
        return jnp.where(edge, unpack(halo3[t], k), found)

    for l in range(layers):
        t, k = l // layers_dev, l % layers_dev
        press = soil_block(t, k)
        store = soil_block(t, layers_dev + k)
        press_a[l] = jnp.where(soil_mask, press, 0.0)
        mid = cond[l]
        up = vertical * 0.5 * (mid + cond[l - 1]) if l > 0 else vertical * 0.5 * mid
        down = vertical * 0.5 * (mid + cond[l + 1]) if l < layers - 1 else vertical * 0.5 * mid
        sides = [lateral * 0.5 * (mid + move(mid)) for move in (north0, south0, east, west)]
        diagonal = store + up + down + sides[0] + sides[1] + sides[2] + sides[3]
        inv = jnp.where(soil_mask, 1.0 / jnp.where(soil_mask, diagonal, 1.0), 0.0)
        inverse[l] = inv
        scaled[l] = jnp.where(soil_mask, store, 0.0) * inv
        coef[0, l] = up * inv
        coef[1, l] = down * inv
        coef[2, l] = jnp.where(first_row, 0.0, sides[0] * inv)
        coef[3, l] = jnp.where(final_row, 0.0, sides[1] * inv)
        coef[4, l] = sides[2] * inv
        coef[5, l] = sides[3] * inv

    def sweep(src, dst):
        for l in range(layers):
            mid = src[l]
            new = rhs[l] + coef[2, l] * north(mid) + coef[3, l] * south(mid)
            new = new + coef[4, l] * east(mid) + coef[5, l] * west(mid)
            if l > 0:
                new = new + coef[0, l] * src[l - 1]
            if l < layers - 1:
                new = new + coef[1, l] * src[l + 1]
            dst[l] = new

    def cycle(c, carry):
        top = press_a[0]
        head = surf[4]
        infil = surf[0] * (head - top)
        evap = surf[1] * jax.nn.sigmoid(top)
        level = head + surf[3]
        flux = surf[5] * north0(level) + surf[6] * south0(level)
        flux = flux + surf[7] * east(level) + surf[8] * west(level) - surf[9] * level
        surf[4] = head + (surf[2] - infil + flux)
        for l in range(layers):
            rhs[l] = scaled[l] * press_a[l]
        rhs[0] = rhs[0] + inverse[0] * (infil - evap)

        def pair(i, inner):
            sweep(press_a, press_b)
            sweep(press_b, press_a)
            return inner

        return lax.fori_loop(0, SWEEPS // 2, pair, carry)

    lax.fori_loop(0, CYCLES, cycle, 0)

    mine = pl.ds(aligned(offset), rows)
    low = lane < own
    half = rows // layers_dev
    final_head = surf[4, mine, :]
    head_pack = jnp.where(
        low[:half],
        pltpu.roll(final_head[:half], LANES - margin, 1),
        pltpu.roll(final_head[half:], margin, 1),
    )
    for t in range(n_sec):
        send_out[t, 0:rows, :] = jnp.where(
            low,
            pltpu.roll(press_a[layers_dev * t, mine, :], LANES - margin, 1),
            pltpu.roll(press_a[layers_dev * t + 1, mine, :], margin, 1),
        )
        send_out[t, rows : rows + half, :] = head_pack

    def result_to(t, source):
        return pltpu.make_async_remote_copy(
            send_out.at[t], recv_out.at[source], out_send.at[t], out_recv.at[source],
            device_id={"sec": t, "gx": g, "gy": h}, device_id_type=MESH,
        )

    for t in range(n_sec):

        @pl.when(s != t)
        def _():
            result_to(t, s).start()

    for t in range(n_sec):

        @pl.when(s == t)
        def _():
            recv_out[t] = send_out[t]

    for when, copy in sends:

        @pl.when(when)
        def _():
            copy().wait_send()

    for t in range(n_sec):

        @pl.when(s != t)
        def _():
            result_to(t, t).wait()

    wide = iota((rows + half, LANES), 1) < own
    for m in range(cols // LANES):
        left, right = recv_out[2 * m], recv_out[2 * m + 1]
        even = jnp.where(wide, left, pltpu.roll(right, own, 1))
        odd = jnp.where(wide, pltpu.roll(left, own, 1), right)
        at = slice(m * LANES, (m + 1) * LANES)
        press_out[0, :, at] = even[:rows]
        press_out[1, :, at] = odd[:rows]
        head_out[0:half, at] = even[rows:]
        head_out[half:rows, at] = odd[rows:]


def shards(*args):
    pressure, soil_embed, geology_embed, conv_weight, out_weight = (args[i] for i in (9, 11, 12, 13, 14))
    n_sec, n_gx, n_gy = (lax.axis_size(name) for name in ("sec", "gx", "gy"))
    layers_dev, rows, cols = pressure.shape
    layers = layers_dev * n_sec
    own = cols // n_sec
    margin = (LANES - own) // 2
    assert margin > REACH and layers_dev * own == LANES and 2 * layers_dev * margin == LANES
    assert (LANES - own - 2 * REACH) * 2 * layers_dev == LANES
    assert n_gx >= 2 and rows >= REACH + 8 and layers_dev == 2
    win_rows = rows + (REACH if n_gx == 2 else 2 * REACH)
    channels = conv_weight.shape[3]
    slots = 16 * pl.cdiv(soil_embed.shape[0], 16) + 16 * pl.cdiv(geology_embed.shape[0], 16)
    depth = TAPS * TAPS * slots
    deep = LANES * pl.cdiv(depth, LANES)
    geom = (n_sec, n_gx, n_gy, rows, cols, layers_dev, win_rows)
    vmem = pltpu.VMEM
    dma = pltpu.SemaphoreType.DMA
    bf16 = jnp.bfloat16
    tall = win_rows + 16
    column = (layers, win_rows, LANES)
    scratch = [
        vmem((4, rows, cols), jnp.int32),
        vmem((5, rows, cols), F32),
        vmem((2 * layers_dev, rows, cols), F32),
        vmem(conv_weight.shape, bf16),
        dma((12,)),
        vmem((2, tall, LANES), F32),
        vmem((6, win_rows, LANES), F32),
        vmem((2, rows, LANES), F32),
        vmem((2, tall, LANES), F32),
        vmem((n_sec, 2 * layers_dev - 1, rows, LANES), F32),
        vmem((n_sec, 2 * layers_dev - 1, win_rows, LANES), F32),
        vmem((2, rows, LANES), F32),
        vmem((n_sec, win_rows, LANES), F32),
        vmem((TAPS, 2, tall, LANES), F32),
        vmem((slots, channels), F32),
        vmem((deep, channels), F32),
        vmem((2 * channels, deep), bf16),
        vmem((tall * TAPS * slots, LANES), bf16),
        vmem(column, F32),
        vmem((6,) + column, F32),
        vmem(column, F32),
        vmem(column, F32),
        vmem(column, F32),
        vmem(column, F32),
        vmem(column, F32),
        vmem((10, win_rows, LANES), F32),
        vmem((n_sec, rows + rows // layers_dev, LANES), F32),
        vmem((n_sec, rows + rows // layers_dev, LANES), F32),
        dma((2,)),
        dma((2,)),
        dma((2,)),
        dma((2,)),
        dma((6,)),
        dma((6,)),
        dma((3 * n_sec,)),
        dma((3 * n_sec,)),
        dma((6,)),
        dma((6 * n_sec,)),
        dma((n_sec,)),
        dma((n_sec,)),
    ]
    return pl.pallas_call(
        functools.partial(kernel, geom),
        out_shape=(
            jax.ShapeDtypeStruct(pressure.shape, F32),
            jax.ShapeDtypeStruct((rows, cols), F32),
        ),
        in_specs=[pl.BlockSpec(memory_space=vmem if k in (11, 12, 14) else pl.ANY) for k in range(len(args))],
        out_specs=(pl.BlockSpec(memory_space=vmem), pl.BlockSpec(memory_space=vmem)),
        scratch_shapes=scratch,
        compiler_params=pltpu.CompilerParams(
            collective_id=0, has_side_effects=True, vmem_limit_bytes=62 * 1024 * 1024
        ),
    )(*args[:14], out_weight.T)


def solution(mesh):
    in_specs = (P("gx", "gy"),) * 9 + (P("sec", "gx", "gy"),) * 2 + (P(),) * 4
    out_specs = (P("sec", "gx", "gy"), P("gx", "gy"))
    return jax.shard_map(shards, mesh=mesh, in_specs=in_specs, out_specs=out_specs, check_vma=False)
```

```python
import functools

import jax
import jax.numpy as jnp
from jax import lax
from jax.experimental import pallas as pl
from jax.experimental.pallas import tpu as pltpu
from jax.sharding import PartitionSpec as P

SWEEPS = 4
CYCLES = 4
REACH = SWEEPS * CYCLES
LANES = 128
TAPS = 3

infil_rate = 0.3
lateral = 1.0
vertical = 0.5
F32 = jnp.float32
MESH = pl.DeviceIdType.MESH


def iota(shape, axis):
    return lax.broadcasted_iota(jnp.int32, shape, axis)


def kernel(
    geom,
    soil_ref,
    geology_ref,
    land_ref,
    river_ref,
    elevation_ref,
    roughness_ref,
    rainfall_ref,
    potential_ref,
    head_ref,
    pressure_ref,
    storage_ref,
    soil_embed_ref,
    geology_embed_ref,
    conv_ref,
    outw_ref,
    press_out,
    head_out,
    whole_in,
    real_in,
    soil_in,
    conv_in,
    in_sems,
    cls,
    fld,
    pack2,
    halo2,
    stage3,
    win3,
    pack3,
    halo3,
    shifted_cls,
    table,
    taps,
    split,
    onehot,
    cond,
    coef,
    scaled,
    inverse,
    press_a,
    press_b,
    rhs,
    surf,
    send_out,
    recv_out,
    cls_send,
    cls_recv,
    fld_send,
    fld_recv,
    p2_send,
    p2_recv,
    s3_send,
    s3_recv,
    p3_send,
    p3_recv,
    out_send,
    out_recv,
):
    n_sec, n_gx, n_gy, rows, cols, layers_dev, win_rows = geom
    layers = n_sec * layers_dev
    own = cols // n_sec
    margin = (LANES - own) // 2
    groups = LANES // margin
    keep = own + 2 * REACH
    low_lane = margin - REACH
    piece = LANES - keep
    s, g, h = (
        jnp.clip(lax.axis_index(name), 0, size - 1) for name, size in (("sec", n_sec), ("gx", n_gx), ("gy", n_gy))
    )
    last = n_sec - 1
    extra = 8
    deep = REACH + extra

    def aligned(value):
        return pl.multiple_of(value, 8)

    offset = REACH * g if n_gx == 2 else REACH

    def exists(dg, dh):
        return (g + dg >= 0) & (g + dg < n_gx) & (h + dh >= 0) & (h + dh < n_gy)

    surface_refs = (
        soil_ref, geology_ref, land_ref, river_ref, elevation_ref, roughness_ref, rainfall_ref, potential_ref, head_ref
    )
    surface_in = [whole_in.at[k] for k in range(4)] + [real_in.at[k] for k in range(5)]
    soil_parts = [soil_in.at[pl.ds(0, layers_dev)], soil_in.at[pl.ds(layers_dev, layers_dev)]]
    loads = [
        pltpu.make_async_copy(src, dst, in_sems.at[k])
        for k, (src, dst) in enumerate(
            zip(
                (*surface_refs, pressure_ref, storage_ref, conv_ref),
                (*surface_in, *soil_parts, conv_in),
            )
        )
    ]
    for load in loads:
        load.start()

    barrier = pltpu.get_barrier_semaphore()
    count = jnp.int32(0)
    for dg in (-1, 0, 1):
        for dh in (-1, 0, 1):
            for t in range(n_sec):
                met = exists(dg, dh)
                if dh == 0 and dg == 0:
                    met = met & (s != t)
                if dh == 1 and t != 0:
                    met = met & (s == last)
                if dh == -1 and t != last:
                    met = met & (s == 0)

                @pl.when(met)
                def _():
                    pl.semaphore_signal(
                        barrier, inc=1, device_id={"sec": t, "gx": g + dg, "gy": h + dh}, device_id_type=MESH
                    )

                count = count + met.astype(jnp.int32)

    for load in loads[:9]:
        load.wait()
    lane = iota((rows, LANES), 1)
    turn = lax.rem(margin - own * s + cols, cols)

    def window_of(values):
        return pltpu.roll(values, turn, 1)[:, :LANES]

    land = whole_in[2].astype(F32)
    rough = land * (1.0 + whole_in[3].astype(F32)) * real_in[1]
    classes = [whole_in[0].astype(F32), whole_in[1].astype(F32)]
    fields = [
        land,
        rough,
        real_in[0],
        land * real_in[2],
        land * real_in[3],
        real_in[4],
    ]
    windows = [window_of(v) for v in classes + fields]
    for k in range(2):
        cls[k, pl.ds(aligned(offset + extra), rows), :] = windows[k]
    for k in range(6):
        fld[k, pl.ds(aligned(offset), rows), :] = windows[2 + k]
    base = jnp.where(s == 0, 0, LANES - margin)
    for b in range(2):
        packed = jnp.zeros((rows, LANES), F32)
        for k in range(groups):
            moved = pltpu.roll(windows[b * groups + k], lax.rem(margin * k - base + LANES, LANES), 1)
            packed = jnp.where((lane >= margin * k) & (lane < margin * (k + 1)), moved, packed)
        pack2[b] = packed

    pl.semaphore_wait(barrier, count)

    def source_rows(dg, size):
        return pl.ds(rows - size if dg == 1 else 0, size)

    def target_rows(dg, pad, size):
        if dg == 0:
            return pl.ds(aligned(offset + pad), size)
        if dg == 1:
            return pl.ds(REACH + pad - size, size)
        return pl.ds((0 if n_gx == 2 else REACH) + rows + pad, size)

    def giver_rows(dg, pad, size):
        if dg == 1:
            return pl.ds((0 if n_gx == 2 else REACH) + pad + rows - size, size)
        return pl.ds(REACH + pad, size)

    sends = []
    recvs = {"first": [], "soil": [], "rest": []}

    def message(kind, send_when, recv_when, src, dst, recv_dst, ssem, rsem, rsem_here, target, giver):
        def copy():
            return pltpu.make_async_remote_copy(src(), dst(), ssem, rsem, device_id=target, device_id_type=MESH)

        def here():
            return pltpu.make_async_remote_copy(
                src(), recv_dst(), ssem, rsem_here, device_id=giver, device_id_type=MESH
            )

        if recv_when is not None:
            recvs[kind].append((recv_when, here))
        if send_when is not None:
            sends.append((send_when, copy))

            @pl.when(send_when)
            def _():
                copy().start()

    def surface_to(kind, dg, ref, pad, size, ssem, rsem):
        i = (dg + 1) // 2
        message(
            kind, exists(dg, 0), exists(-dg, 0),
            lambda: ref.at[:, giver_rows(dg, pad, size), :],
            lambda: ref.at[:, target_rows(dg, pad, size), :],
            lambda: ref.at[:, target_rows(dg, pad, size), :],
            ssem.at[i], rsem.at[i], rsem.at[i],
            {"sec": s, "gx": g + dg, "gy": h},
            {"sec": s, "gx": g - dg, "gy": h},
        )

    for dg in (-1, 1):
        surface_to("first", dg, cls, extra, deep, cls_send, cls_recv)

    def corner_to(side, dh, keeper, dg):
        size = rows if dg == 0 else deep
        j = dg + 1
        message(
            "first", exists(dg, dh) & (s == keeper), exists(-dg, -dh) & (s == keeper),
            lambda: pack2.at[:, source_rows(dg, size), :],
            lambda: halo2.at[:, target_rows(dg, extra, size), :],
            lambda: halo2.at[:, target_rows(dg, extra, size), :],
            p2_send.at[side * 3 + j], p2_recv.at[side * 3 + j], p2_recv.at[side * 3 + j],
            {"sec": s, "gx": g + dg, "gy": h + dh},
            {"sec": s, "gx": g - dg, "gy": h - dh},
        )

    for side, (dh, keeper) in enumerate(((1, 0), (-1, last))):
        for dg in (-1, 0, 1):
            corner_to(side, dh, keeper, dg)

    for dg in (-1, 1):
        surface_to("rest", dg, fld, 0, REACH, fld_send, fld_recv)

    loads[9].wait()
    loads[10].wait()
    soil_blocks = [soil_in[k] for k in range(2 * layers_dev)]
    n_blocks = len(soil_blocks)
    sides3 = {0: (0, 0), last: (1, LANES - margin)}
    for t in range(n_sec):
        blocks = [pltpu.roll(v, (margin - own * t) % cols, 1)[:, :LANES] for v in soil_blocks]
        for j in range(n_blocks - 1):
            moved = pltpu.roll(blocks[-1], (keep - piece * j) % LANES, 1)
            stage3[t, j] = jnp.where((lane >= low_lane) & (lane < low_lane + keep), blocks[j], moved)
        if t in sides3:
            side, edge = sides3[t]
            packed = jnp.zeros((rows, LANES), F32)
            for k in range(n_blocks):
                moved = pltpu.roll(blocks[k], (margin * k - edge) % LANES, 1)
                packed = jnp.where((lane >= margin * k) & (lane < margin * (k + 1)), moved, packed)
            pack3[side] = packed
    for t in range(n_sec):

        @pl.when(s == t)
        def _():
            for j in range(n_blocks - 1):
                win3[t, j, pl.ds(aligned(offset), rows), :] = stage3[t, j]

    def soil_to(dg, t):
        way = (dg + 1) * n_sec
        size = rows if dg == 0 else REACH
        message(
            "soil", exists(dg, 0) if dg else (s != t), exists(-dg, 0) if dg else (s != t),
            lambda: stage3.at[t, :, source_rows(dg, size), :],
            lambda: win3.at[s, :, target_rows(dg, 0, size), :],
            lambda: win3.at[t, :, target_rows(dg, 0, size), :],
            s3_send.at[way + t], s3_recv.at[way + s], s3_recv.at[way + t],
            {"sec": t, "gx": g + dg, "gy": h},
            {"sec": t, "gx": g - dg, "gy": h},
        )

    for dg in (-1, 1, 0):
        for t in range(n_sec):
            soil_to(dg, t)

    def soil_edge_to(side, dh, keeper, dg, t):
        way = side * 3 + dg + 1
        size = rows if dg == 0 else REACH
        message(
            "soil", exists(dg, dh) if t == 0 else None, exists(-dg, -dh) & (s == keeper),
            lambda: pack3.at[side, source_rows(dg, size), :],
            lambda: halo3.at[s, target_rows(dg, 0, size), :],
            lambda: halo3.at[t, target_rows(dg, 0, size), :],
            p3_send.at[way], p3_recv.at[way * n_sec + s], p3_recv.at[way * n_sec + t],
            {"sec": keeper, "gx": g + dg, "gy": h + dh},
            {"sec": t, "gx": g - dg, "gy": h - dh},
        )

    for side, (dh, keeper) in enumerate(((1, 0), (-1, last))):
        for dg in (0, -1, 1):
            for t in range(n_sec):
                soil_edge_to(side, dh, keeper, dg, t)

    def wait_all(kind):
        for when, copy in recvs[kind]:

            @pl.when(when)
            def _():
                copy().wait_recv()

    soil_slots = 16 * pl.cdiv(soil_embed_ref.shape[0], 16)
    geo_slots = 16 * pl.cdiv(geology_embed_ref.shape[0], 16)
    slots = soil_slots + geo_slots
    table[...] = jnp.zeros(table.shape, F32)
    table[0 : soil_embed_ref.shape[0], :] = soil_embed_ref[...].astype(F32)
    table[soil_slots : soil_slots + geology_embed_ref.shape[0], :] = geology_embed_ref[...].astype(F32)
    embed = table[...].astype(jnp.bfloat16)
    loads[11].wait()
    taps[...] = jnp.zeros(taps.shape, F32)
    for i in range(TAPS):
        for j in range(TAPS):
            at = (i * TAPS + j) * slots
            taps[at : at + slots, :] = jnp.dot(embed, conv_in[i, j], preferred_element_type=F32)
    channels = conv_ref.shape[3]
    depth = TAPS * TAPS * slots
    for k in range(taps.shape[0] // LANES):
        turned = taps[k * LANES : (k + 1) * LANES, :].T
        upper = turned.astype(jnp.bfloat16)
        split[0:channels, k * LANES : (k + 1) * LANES] = upper
        split[channels : 2 * channels, k * LANES : (k + 1) * LANES] = (turned - upper.astype(F32)).astype(
            jnp.bfloat16
        )
    outw_t = outw_ref[...]

    wait_all("first")

    edge_at = jnp.where(s == 0, 0, LANES - margin)

    def edge_mask(shape):
        at = iota(shape, 1)
        return ((s == 0) & (at < margin)) | ((s == last) & (at >= LANES - margin))

    def on_grid(shape, first):
        row = g * rows - offset + first + iota(shape, 0)
        col = h * cols + s * own - margin + iota(shape, 1)
        return (row >= 0) & (row < n_gx * rows) & (col >= 0) & (col < n_gy * cols)

    def unpack(packed, k):
        return pltpu.roll(packed, lax.rem(edge_at - margin * k + LANES, LANES), 1)

    tall = (win_rows + 2 * extra, LANES)
    tall_edge = edge_mask(tall)
    tall_grid = on_grid(tall, -extra)
    for k in range(2):
        merged = jnp.where(tall_edge, unpack(halo2[0], k), cls[k])
        merged = jnp.where(tall_grid, merged, -100.0)
        for j in range(TAPS):
            shifted_cls[j, k] = merged if j == 1 else pltpu.roll(merged, (1 - j) % LANES, 1)

    group = 8

    def make_onehot(it, carry):
        for j in range(TAPS):
            soil_rows = shifted_cls[j, 0, pl.ds(aligned(it * group), group), :]
            geo_rows = shifted_cls[j, 1, pl.ds(aligned(it * group), group), :]
            for k in range(group):
                at = pl.multiple_of(((it * group + k) * TAPS + j) * slots, 16)
                soil_hot = iota((soil_slots, LANES), 0).astype(F32) == soil_rows[k : k + 1]
                geo_hot = iota((geo_slots, LANES), 0).astype(F32) == geo_rows[k : k + 1]
                hot = jnp.concatenate([soil_hot, geo_hot], axis=0)
                onehot[pl.ds(at, slots), :] = jnp.where(hot, 1.0, 0.0).astype(jnp.bfloat16)
        return carry

    lax.fori_loop(0, tall[0] // group, make_onehot, 0)

    def convolve(it, carry):
        r = it * group
        parts = [
            onehot[pl.ds(pl.multiple_of((r + k + extra - 1) * TAPS * slots, 16), depth), :] for k in range(group)
        ]
        both = jnp.dot(split[:, :depth], jnp.concatenate(parts, axis=1), preferred_element_type=F32)
        hidden = jnp.maximum(both[:channels] + both[channels:], 0.0).astype(jnp.bfloat16)
        found = jnp.dot(outw_t, hidden, preferred_element_type=F32)
        stacked = jnp.stack([found[:, k * LANES : (k + 1) * LANES] for k in range(group)], axis=0)
        cond[:, pl.ds(aligned(r), group), :] = jnp.swapaxes(stacked, 0, 1)
        return carry

    lax.fori_loop(0, win_rows // group, convolve, 0)

    flat = (win_rows, LANES)
    grid_mask = on_grid(flat, 0)
    edge = edge_mask(flat)
    row_at = iota(flat, 0)
    lane_at = iota(flat, 1)
    usable = grid_mask & (lane_at > 0) & (lane_at < LANES - 1)
    for l in range(layers):
        cond[l] = jnp.where(usable, jnp.exp(cond[l]), 0.0)

    def north(v):
        return pltpu.roll(v, 1, 0)

    def south(v):
        return pltpu.roll(v, win_rows - 1, 0)

    def east(v):
        return pltpu.roll(v, LANES - 1, 1)

    def west(v):
        return pltpu.roll(v, 1, 1)

    first_row = row_at == 0
    final_row = row_at == win_rows - 1

    def north0(v):
        return jnp.where(first_row, 0.0, north(v))

    def south0(v):
        return jnp.where(final_row, 0.0, south(v))

    wait_all("rest")

    def field(k):
        b, at = (k + 2) // groups, (k + 2) % groups
        merged = jnp.where(edge, unpack(halo2[b, extra : extra + win_rows, :], at), fld[k])
        return jnp.where(grid_mask, merged, 0.0)

    land_w, rough_w, elev_w, rain_w, potential_w, head_w = [field(k) for k in range(6)]
    top_cond = cond[0]
    surf[0] = land_w * (infil_rate * top_cond / (1.0 + top_cond))
    surf[1] = potential_w
    surf[2] = rain_w
    surf[3] = elev_w
    surf[4] = head_w
    total = jnp.zeros(flat, F32)
    for k, move in enumerate((north0, south0, east, west)):
        way = land_w * 0.5 * (rough_w + move(rough_w))
        total = total + way
        surf[5 + k] = way
    surf[9] = total

    wait_all("soil")

    soil_mask = grid_mask & (lane_at >= low_lane) & (lane_at < low_lane + keep)

    def soil_block(t, k):
        if k < n_blocks - 1:
            found = win3[t, k]
        else:
            found = pltpu.roll(win3[t, 0], (-keep) % LANES, 1)
            for j in range(1, n_blocks - 1):
                back = pltpu.roll(win3[t, j], (piece * j - keep) % LANES, 1)
                found = jnp.where(lane_at < low_lane + piece * j, found, back)
        return jnp.where(edge, unpack(halo3[t], k), found)

    for l in range(layers):
        t, k = l // layers_dev, l % layers_dev
        press = soil_block(t, k)
        store = soil_block(t, layers_dev + k)
        press_a[l] = jnp.where(soil_mask, press, 0.0)
        mid = cond[l]
        up = vertical * 0.5 * (mid + cond[l - 1]) if l > 0 else vertical * 0.5 * mid
        down = vertical * 0.5 * (mid + cond[l + 1]) if l < layers - 1 else vertical * 0.5 * mid
        sides = [lateral * 0.5 * (mid + move(mid)) for move in (north0, south0, east, west)]
        diagonal = store + up + down + sides[0] + sides[1] + sides[2] + sides[3]
        inv = jnp.where(soil_mask, 1.0 / jnp.where(soil_mask, diagonal, 1.0), 0.0)
        inverse[l] = inv
        scaled[l] = jnp.where(soil_mask, store, 0.0) * inv
        coef[0, l] = up * inv
        coef[1, l] = down * inv
        coef[2, l] = jnp.where(first_row, 0.0, sides[0] * inv)
        coef[3, l] = jnp.where(final_row, 0.0, sides[1] * inv)
        coef[4, l] = sides[2] * inv
        coef[5, l] = sides[3] * inv

    def sweep(src, dst):
        for l in range(layers):
            mid = src[l]
            new = rhs[l] + coef[2, l] * north(mid) + coef[3, l] * south(mid)
            new = new + coef[4, l] * east(mid) + coef[5, l] * west(mid)
            if l > 0:
                new = new + coef[0, l] * src[l - 1]
            if l < layers - 1:
                new = new + coef[1, l] * src[l + 1]
            dst[l] = new

    def cycle(c, carry):
        top = press_a[0]
        head = surf[4]
        infil = surf[0] * (head - top)
        evap = surf[1] * jax.nn.sigmoid(top)
        level = head + surf[3]
        flux = surf[5] * north0(level) + surf[6] * south0(level)
        flux = flux + surf[7] * east(level) + surf[8] * west(level) - surf[9] * level
        surf[4] = head + (surf[2] - infil + flux)
        for l in range(layers):
            rhs[l] = scaled[l] * press_a[l]
        rhs[0] = rhs[0] + inverse[0] * (infil - evap)

        def pair(i, inner):
            sweep(press_a, press_b)
            sweep(press_b, press_a)
            return inner

        return lax.fori_loop(0, SWEEPS // 2, pair, carry)

    lax.fori_loop(0, CYCLES, cycle, 0)

    mine = pl.ds(aligned(offset), rows)
    low = lane < own
    half = rows // layers_dev
    final_head = surf[4, mine, :]
    head_pack = jnp.where(
        low[:half],
        pltpu.roll(final_head[:half], LANES - margin, 1),
        pltpu.roll(final_head[half:], margin, 1),
    )
    for t in range(n_sec):
        send_out[t, 0:rows, :] = jnp.where(
            low,
            pltpu.roll(press_a[layers_dev * t, mine, :], LANES - margin, 1),
            pltpu.roll(press_a[layers_dev * t + 1, mine, :], margin, 1),
        )
        send_out[t, rows : rows + half, :] = head_pack

    def result_to(t, source):
        return pltpu.make_async_remote_copy(
            send_out.at[t], recv_out.at[source], out_send.at[t], out_recv.at[source],
            device_id={"sec": t, "gx": g, "gy": h}, device_id_type=MESH,
        )

    for t in range(n_sec):

        @pl.when(s != t)
        def _():
            result_to(t, s).start()

    for t in range(n_sec):

        @pl.when(s == t)
        def _():
            recv_out[t] = send_out[t]

    for when, copy in sends:

        @pl.when(when)
        def _():
            copy().wait_send()

    for t in range(n_sec):

        @pl.when(s != t)
        def _():
            result_to(t, t).wait()

    wide = iota((rows + half, LANES), 1) < own
    for m in range(cols // LANES):
        left, right = recv_out[2 * m], recv_out[2 * m + 1]
        even = jnp.where(wide, left, pltpu.roll(right, own, 1))
        odd = jnp.where(wide, pltpu.roll(left, own, 1), right)
        at = slice(m * LANES, (m + 1) * LANES)
        press_out[0, :, at] = even[:rows]
        press_out[1, :, at] = odd[:rows]
        head_out[0:half, at] = even[rows:]
        head_out[half:rows, at] = odd[rows:]


def shards(*args):
    pressure, soil_embed, geology_embed, conv_weight, out_weight = (args[i] for i in (9, 11, 12, 13, 14))
    n_sec, n_gx, n_gy = (lax.axis_size(name) for name in ("sec", "gx", "gy"))
    layers_dev, rows, cols = pressure.shape
    layers = layers_dev * n_sec
    own = cols // n_sec
    margin = (LANES - own) // 2
    assert margin > REACH and layers_dev * own == LANES and 2 * layers_dev * margin == LANES
    assert (LANES - own - 2 * REACH) * 2 * layers_dev == LANES
    assert n_gx >= 2 and rows >= REACH + 8 and layers_dev == 2
    win_rows = rows + (REACH if n_gx == 2 else 2 * REACH)
    channels = conv_weight.shape[3]
    slots = 16 * pl.cdiv(soil_embed.shape[0], 16) + 16 * pl.cdiv(geology_embed.shape[0], 16)
    depth = TAPS * TAPS * slots
    deep = LANES * pl.cdiv(depth, LANES)
    geom = (n_sec, n_gx, n_gy, rows, cols, layers_dev, win_rows)
    vmem = pltpu.VMEM
    dma = pltpu.SemaphoreType.DMA
    bf16 = jnp.bfloat16
    tall = win_rows + 16
    column = (layers, win_rows, LANES)
    scratch = [
        vmem((4, rows, cols), jnp.int32),
        vmem((5, rows, cols), F32),
        vmem((2 * layers_dev, rows, cols), F32),
        vmem(conv_weight.shape, bf16),
        dma((12,)),
        vmem((2, tall, LANES), F32),
        vmem((6, win_rows, LANES), F32),
        vmem((2, rows, LANES), F32),
        vmem((2, tall, LANES), F32),
        vmem((n_sec, 2 * layers_dev - 1, rows, LANES), F32),
        vmem((n_sec, 2 * layers_dev - 1, win_rows, LANES), F32),
        vmem((2, rows, LANES), F32),
        vmem((n_sec, win_rows, LANES), F32),
        vmem((TAPS, 2, tall, LANES), F32),
        vmem((slots, channels), F32),
        vmem((deep, channels), F32),
        vmem((2 * channels, deep), bf16),
        vmem((tall * TAPS * slots, LANES), bf16),
        vmem(column, F32),
        vmem((6,) + column, F32),
        vmem(column, F32),
        vmem(column, F32),
        vmem(column, F32),
        vmem(column, F32),
        vmem(column, F32),
        vmem((10, win_rows, LANES), F32),
        vmem((n_sec, rows + rows // layers_dev, LANES), F32),
        vmem((n_sec, rows + rows // layers_dev, LANES), F32),
        dma((2,)),
        dma((2,)),
        dma((2,)),
        dma((2,)),
        dma((6,)),
        dma((6,)),
        dma((3 * n_sec,)),
        dma((3 * n_sec,)),
        dma((6,)),
        dma((6 * n_sec,)),
        dma((n_sec,)),
        dma((n_sec,)),
    ]
    return pl.pallas_call(
        functools.partial(kernel, geom),
        out_shape=(
            jax.ShapeDtypeStruct(pressure.shape, F32),
            jax.ShapeDtypeStruct((rows, cols), F32),
        ),
        in_specs=[pl.BlockSpec(memory_space=vmem if k in (11, 12, 14) else pl.ANY) for k in range(len(args))],
        out_specs=(pl.BlockSpec(memory_space=vmem), pl.BlockSpec(memory_space=vmem)),
        scratch_shapes=scratch,
        compiler_params=pltpu.CompilerParams(
            collective_id=0, has_side_effects=True, vmem_limit_bytes=62 * 1024 * 1024
        ),
    )(*args[:14], out_weight.T)


def solution(mesh):
    in_specs = (P("gx", "gy"),) * 9 + (P("sec", "gx", "gy"),) * 2 + (P(),) * 4
    out_specs = (P("sec", "gx", "gy"), P("gx", "gy"))
    return jax.shard_map(shards, mesh=mesh, in_specs=in_specs, out_specs=out_specs, check_vma=False)
```
